32 devices in a mesh: dp: 8 (over z, core), mp: 4 (over y, x).
Axes of the slice: x: 2, y: 2, z: 4, core: 2. Of those that a mesh axis runs over, the one named last changes fastest.
Arguments:
- picture_summary_vectors: bfloat16 [4096, 1152], P(('dp', 'mp')), may hold values from -6 to 6
- caption_summary_vectors: bfloat16 [4096, 1152], P(('dp', 'mp')), may hold values from -6 to 6
- picture_mapping_matrix: bfloat16 [1152, 1152], P(('dp', 'mp')), may hold values from -0.1875 to 0.1875
- caption_mapping_matrix: bfloat16 [1152, 1152], P(('dp', 'mp')), may hold values from -0.1875 to 0.1875
- picture_partner_label: int32 [4096], P(('dp', 'mp')), may hold values from 0 to 1023
- caption_partner_label: int32 [4096], P(('dp', 'mp')), may hold values from 0 to 1023
- similarity_factor: float32 [1], replicated, may hold values from 5 to 15
- offset_term: float32 [1], replicated, may hold values from -4 to -1
Outputs:
- img_grad: bfloat16 [4096, 1152], P(('dp', 'mp'))
- txt_grad: bfloat16 [4096, 1152], P(('dp', 'mp'))
- w_img_grad: float32 [1152, 1152], P(('dp', 'mp'))
- w_txt_grad: float32 [1152, 1152], P(('dp', 'mp'))
The draws below stay inside these ranges and needn't reach their ends.
All inputs are finite; a program needn't handle non-finite values.
Results may differ from the reference program's by a relative error of at most 0.023.
Values may be sent and summed in bfloat16 or wider, within the bound.
A program may use at most 128 MiB of HBM per device.

```python
import math
import jax
import jax.numpy as jnp
from jax import lax

D = 1152
E = 1152
B = 4096


def place_ends(values, own_key, least, top_value):
    index_at = [jax.random.randint(jax.random.fold_in(own_key, axis), (), 0, length) for axis, length in enumerate(values.shape)]
    widest = values.shape.index(max(values.shape))
    neighbour = index_at[:widest] + [(index_at[widest] + 1) % values.shape[widest]] + index_at[widest + 1:]
    return values.at[tuple(index_at)].set(least).at[tuple(neighbour)].set(top_value)


def shard_levels(stream_key, dims, cuts, smallest, top_value):
    level, own = 1.0, jax.random.fold_in(stream_key, 6)
    for dim, blocks in cuts:
        heights = jnp.exp(jax.random.uniform(jax.random.fold_in(own, dim), (blocks,), jnp.float32, smallest / len(cuts), top_value / len(cuts)))
        level = level * jnp.repeat(heights, dims[dim] // blocks).reshape([-1 if axis == dim else 1 for axis in range(len(dims))])
    return level


def normal_values(key, extent, scale, most, cuts=(), held_as=jnp.bfloat16):
    result = jax.random.normal(key, extent, jnp.float32) * scale
    if len(cuts) > 0:
        result = shard_levels(key, extent, cuts, -0.22, 0.18) * result
    return jnp.clip(result, min=-most, max=most).astype(held_as)


def setup_inputs(seed: int = 0) -> dict:
    key_list = jax.random.split(jax.random.key(seed), 9)
    picture_summary_vectors = normal_values(key_list[0], (B, D), 1.0, 6.0, ((0, 32),))
    caption_summary_vectors = normal_values(key_list[1], (B, D), 1.0, 6.0, ((0, 32),))
    picture_mapping_matrix = normal_values(key_list[2], (D, E), D ** -0.5, 0.1875, ((0, 32),))
    caption_mapping_matrix = normal_values(key_list[3], (D, E), D ** -0.5, 0.1875, ((0, 32),))
    picture_partner_label = place_ends(jax.random.randint(key_list[4], (B,), 0, B // 4), jax.random.fold_in(key_list[4], 1), 0, (B // 4) - 1).astype(jnp.int32)
    caption_partner_label = place_ends(jax.random.randint(key_list[5], (B,), 0, B // 4), jax.random.fold_in(key_list[5], 1), 0, (B // 4) - 1).astype(jnp.int32)
    similarity_factor = jnp.clip(jax.random.uniform(key_list[6], (1,), jnp.float32, 5.0, 15.0), 5.0, 15.0)
    offset_term = jnp.clip(jax.random.uniform(key_list[7], (1,), jnp.float32, -4.0, -1.0), -4.0, -1.0)
    return {"picture_summary_vectors": picture_summary_vectors, "caption_summary_vectors": caption_summary_vectors, "picture_mapping_matrix": picture_mapping_matrix, "caption_mapping_matrix": caption_mapping_matrix, "picture_partner_label": picture_partner_label, "caption_partner_label": caption_partner_label, "similarity_factor": similarity_factor, "offset_term": offset_term}


def embed(feat, weight):
    pre = jnp.dot(feat, weight, preferred_element_type=jnp.float32)
    radius = jnp.sqrt(lax.optimization_barrier(jnp.sum(pre * pre, axis=1, keepdims=True)) + 1e-06)
    return (pre / radius, radius)

def backward_rows(unit, radius, grad, feat, weight):
    d_pre = ((grad - unit * lax.optimization_barrier(jnp.sum(unit * grad, axis=1, keepdims=True))) / radius).astype(jnp.bfloat16)
    d_feat = lax.dot_general(d_pre, weight, (((1,), (1,)), ((), ())), preferred_element_type=jnp.float32).astype(jnp.bfloat16)
    d_weight = lax.dot_general(feat, d_pre, (((0,), (0,)), ((), ())), preferred_element_type=jnp.float32)
    return (d_feat, d_weight)

def reference(picture_summary_vectors, caption_summary_vectors, picture_mapping_matrix, caption_mapping_matrix, picture_partner_label, caption_partner_label, similarity_factor, offset_term):
    unit_img, rad_img = embed(picture_summary_vectors, picture_mapping_matrix)
    unit_txt, rad_txt = embed(caption_summary_vectors, caption_mapping_matrix)
    emb_img = unit_img.astype(jnp.bfloat16)
    emb_txt = unit_txt.astype(jnp.bfloat16)
    similarity_multiplier = similarity_factor[0]
    offset = offset_term[0]
    block = math.gcd(B, 1024)
    width = emb_img.shape[1]
    blocks_emb = emb_img.reshape(B // block, block, width)
    blocks_ids = picture_partner_label.reshape(B // block, block)

    def visit(total, item):
        emb_block, ids_block = item
        logits = similarity_multiplier * lax.dot_general(emb_block, emb_txt, (((1,), (1,)), ((), ())), preferred_element_type=jnp.float32) + offset
        sign = jnp.where(ids_block[:, None] == caption_partner_label[None, :], 1.0, -1.0).astype(jnp.float32)
        slope = (-sign * jax.nn.sigmoid(-sign * logits)).astype(jnp.bfloat16)
        image_part = similarity_multiplier * jnp.dot(slope, emb_txt, preferred_element_type=jnp.float32)
        total = total + lax.dot_general(slope, emb_block, (((0,), (0,)), ((), ())), preferred_element_type=jnp.float32)
        return (total, image_part)
    start = jnp.zeros((B, width), jnp.float32)
    total, parts = lax.scan(visit, start, (blocks_emb, blocks_ids))
    d_emb_img = parts.reshape(B, width)
    d_emb_txt = similarity_multiplier * total
    img_grad, w_img_grad = backward_rows(unit_img, rad_img, d_emb_img, picture_summary_vectors, picture_mapping_matrix)
    txt_grad, w_txt_grad = backward_rows(unit_txt, rad_txt, d_emb_txt, caption_summary_vectors, caption_mapping_matrix)
    return (img_grad, txt_grad, w_img_grad, w_txt_grad)
```

```python
import functools
import math

import jax
import jax.numpy as jnp
from jax import lax
from jax.experimental import pallas as pl
from jax.experimental.pallas import tpu as pltpu
from jax.sharding import PartitionSpec as P

MESH = pl.DeviceIdType.MESH
TXT, IMG = 0, 1
F32, BF16 = jnp.float32, jnp.bfloat16


def dot(a, b, da, db):
    return lax.dot_general(a, b, (((da,), (db,)), ((), ())), preferred_element_type=F32)


def loop(low, high, body):
    def step(i, carry):
        body(i)
        return carry

    lax.fori_loop(low, high, step, 0)


def kernel(
    nz, nm, rows, wrows,
    ximg, xtxt, wimg, wtxt, idimg, idtxt, sim_ref, off_ref,
    gimg, gtxt, dwimg, dwtxt,
    wbuf, wfull, fs, xt, unit, rad, dpre, imgs, txts, iids, tids, slopes,
    dt, tcs, tcr, tzs, tzr, dis, dir_, gown,
    rcs, rcr, rxs, rxr, rzs, rzr, rown,
    wz_s, wz_r, wx_s, wx_r, wc_s, wc_r,
    ii_s, ii_r, ti_s, ti_r, tj_s, tj_r,
    im_s, im_r, tx_s, tx_r, ty_s, ty_r,
    tc_s, tc_r, tz_s, tz_r, di_s, di_r,
    rc_s, rc_r, rx_s, rx_r, rz_s, rz_r,
):
    dp, m = lax.axis_index("dp"), lax.axis_index("mp")
    z, c = lax.div(dp, 2), lax.rem(dp, 2)
    other = 1 - c
    big = nm * wrows
    group = fs.shape[0] // big
    x_refs, w_refs = (xtxt, ximg), (wtxt, wimg)

    def zat(k):
        return lax.rem(z - k + nz, nz)

    def zto(k):
        return lax.rem(z + k, nz)

    def mat(k):
        return lax.rem(m - k + nm, nm)

    def mto(k):
        return lax.rem(m + k, nm)

    core = (2 * z + other, m)

    def copy(src, dst, s, r, dev):
        return pltpu.make_async_remote_copy(
            src_ref=src, dst_ref=dst, send_sem=s, recv_sem=r, device_id=dev, device_id_type=MESH
        )

    barrier = pltpu.get_barrier_semaphore()
    for k in range(1, nz):
        pl.semaphore_signal(barrier, inc=1, device_id=(2 * zto(k) + c, m), device_id_type=MESH)
    for k in range(1, nm):
        pl.semaphore_signal(barrier, inc=1, device_id=(dp, mto(k)), device_id_type=MESH)
    pl.semaphore_signal(barrier, inc=1, device_id=core, device_id_type=MESH)
    pl.semaphore_wait(barrier, nz + nm - 1)

    def w_z(w, k):
        return copy(w_refs[w], wbuf.at[w, dp, m], wz_s.at[w, k], wz_r.at[w, k], (2 * zto(k) + c, m))

    def w_x(w, k, j):
        slot = wbuf.at[w, 2 * zat(k) + c, m]
        return copy(slot, slot, wx_s.at[w, k, j], wx_r.at[w, k, j], (dp, mto(j)))

    def w_c(w, k, j):
        slot = wbuf.at[w, 2 * zat(k) + c, mat(j)]
        return copy(slot, slot, wc_s.at[w, k, j], wc_r.at[w, k, j], core)

    def w_z_wait(w, k):
        slot = wbuf.at[w, 2 * zat(k) + c, m]
        copy(slot, slot, wz_s.at[w, k], wz_r.at[w, k], core).wait_recv()

    def w_x_wait(w, k, j):
        slot = wbuf.at[w, 2 * zat(k) + c, mat(j)]
        copy(slot, slot, wx_s.at[w, k, j], wx_r.at[w, k, j], core).wait_recv()

    def w_c_wait(w, k, j):
        slot = wbuf.at[w, 2 * zat(k) + other, mat(j)]
        copy(slot, slot, wc_s.at[w, k, j], wc_r.at[w, k, j], core).wait_recv()

    def w_start(w):
        for k in range(1, nz):
            w_z(w, k).start()
        wbuf[w, dp, m] = w_refs[w][...]
        for j in range(1, nm):
            w_x(w, 0, j).start()
        w_c(w, 0, 0).start()

    def w_pass_z(w):
        def body(k):
            w_z_wait(w, k)
            for j in range(1, nm):
                w_x(w, k, j).start()
            w_c(w, k, 0).start()

        loop(1, nz, body)

    def w_pass_x(w):
        def body(k):
            for j in range(1, nm):
                w_x_wait(w, k, j)
                w_c(w, k, j).start()

        loop(0, nz, body)

    def w_finish(w):
        def body(k):
            for j in range(nm):
                w_c_wait(w, k, j)

        loop(0, nz, body)

        def join(g):
            for n in range(group * nm):
                d = g * group + n // nm
                fs[n * wrows:(n + 1) * wrows, :] = wbuf[w, d, n % nm].astype(F32)
            wfull[w, pl.ds(pl.multiple_of(g * group * big, 16), group * big), :] = fs[...].astype(BF16)

        loop(0, 2 * nz // group, join)

    def embed(w):
        pre = dot(x_refs[w][...], wfull[w], 1, 0)
        radius = jnp.sqrt(jnp.sum(pre * pre, axis=1, keepdims=True) + 1e-06)
        out = pre / radius
        unit[w] = out
        rad[w] = radius
        return out.astype(BF16)

    def my(n):
        return pl.ds(pl.multiple_of(n * rows, rows), rows)

    def ids_img(j):
        return copy(idimg, iids.at[m], ii_s.at[j], ii_r.at[j], (dp, mto(j)))

    def ids_txt(k):
        return copy(idtxt, tids.at[dp], ti_s.at[k], ti_r.at[k], (2 * zto(k) + c, m))

    def ids_core(k):
        slot = tids.at[2 * zat(k) + c]
        return copy(slot, slot, tj_s.at[k], tj_r.at[k], core)

    def img_x(j):
        slot = imgs.at[my(m), :]
        return copy(slot, slot, im_s.at[j], im_r.at[j], (dp, mto(j)))

    def txt_z(k):
        slot = txts.at[my(dp), :]
        return copy(slot, slot, tx_s.at[k], tx_r.at[k], (2 * zto(k) + c, m))

    def txt_c(k):
        slot = txts.at[my(2 * zat(k) + c), :]
        return copy(slot, slot, ty_s.at[k], ty_r.at[k], core)

    w_start(TXT)
    iids[m] = idimg[...]
    tids[dp] = idtxt[...]
    for j in range(1, nm):
        ids_img(j).start()
    for k in range(1, nz):
        ids_txt(k).start()
    ids_core(0).start()
    w_pass_z(TXT)
    w_start(IMG)
    for k in range(1, nz):
        slot = tids.at[2 * zat(k) + c]
        copy(slot, slot, ti_s.at[k], ti_r.at[k], core).wait_recv()
        ids_core(k).start()
    for w in (TXT, IMG):
        turned = x_refs[w][...].T if group == 1 else x_refs[w][...].astype(F32).T
        for d in range(2 * nz):
            xt[w, d] = turned[d * big:(d + 1) * big, :].astype(BF16)
    w_pass_x(TXT)
    w_pass_z(IMG)
    w_finish(TXT)
    txts[my(dp), :] = embed(TXT)
    txt_c(0).start()
    for k in range(1, nz):
        txt_z(k).start()
    w_pass_x(IMG)
    w_finish(IMG)
    imgs[my(m), :] = embed(IMG)
    for j in range(1, nm):
        img_x(j).start()

    for j in range(1, nm):
        slot = iids.at[mat(j)]
        copy(slot, slot, ii_s.at[j], ii_r.at[j], core).wait_recv()
    for k in range(nz):
        slot = tids.at[2 * zat(k) + other]
        copy(slot, slot, tj_s.at[k], tj_r.at[k], core).wait_recv()
    for j in range(1, nm):
        slot = imgs.at[my(mat(j)), :]
        copy(slot, slot, im_s.at[j], im_r.at[j], core).wait_recv()

    sim, off = sim_ref[0], off_ref[0]

    def grad_core(k):
        return copy(tcs.at[k], tcr.at[k], tc_s.at[k], tc_r.at[k], core)

    def grad_z(k):
        return copy(tzs.at[k], tzr.at[k], tz_s.at[k], tz_r.at[k], (2 * zat(k) + c, m))

    def pair(k):
        zs = zat(k)

        @pl.when(k > 0)
        def _():
            slot = txts.at[my(2 * zs + c), :]
            copy(slot, slot, tx_s.at[k], tx_r.at[k], core).wait_recv()
            txt_c(k).start()

        slot = txts.at[my(2 * zs + other), :]
        copy(slot, slot, ty_s.at[k], ty_r.at[k], core).wait_recv()
        span = pl.ds(pl.multiple_of(zs * 2 * rows, 2 * rows), 2 * rows)
        idrow = jnp.concatenate([tids[2 * zs][:1], tids[2 * zs + 1][:1]], axis=1)

        def block(q):
            here = my(q)
            logits = sim * dot(imgs[here, :], txts[span, :], 1, 1) + off
            idcol = iids[q].T[:, :1]
            sign = jnp.where(idcol == idrow, 1.0, -1.0).astype(F32)
            slopes[here, span] = (-sign * jax.nn.sigmoid(-sign * logits)).astype(BF16)

        loop(0, nm, block)
        for h in range(2):
            cols = pl.ds(pl.multiple_of(zs * 2 * rows + h * rows, rows), rows)
            dt[h] = dot(slopes[:, cols], imgs[...], 0, 0)
        tcs[k] = dt[other].astype(BF16)
        grad_core(k).start()
        grad_core(k).wait_recv()

        @pl.when(k > 0)
        def _():
            tzs[k] = (dt[c] + tcr[k].astype(F32)).astype(BF16)
            grad_z(k).start()

        @pl.when(k == 0)
        def _():
            gown[TXT] = dt[c] + tcr[k].astype(F32)

    loop(0, nz, pair)

    def grad_img(j):
        return copy(dis.at[j], dir_.at[j], di_s.at[j], di_r.at[j], (dp, mto(j)))

    def img_part(j):
        part = dot(slopes[my(mto(j)), :], txts[...], 1, 0)

        @pl.when(j < nm)
        def _():
            dis[j] = part.astype(BF16)
            grad_img(j).start()

        @pl.when(j == nm)
        def _():
            gown[IMG] = part

    loop(1, nm + 1, img_part)

    def rs_core(w, k):
        return copy(rcs.at[w, k], rcr.at[w, k], rc_s.at[w, k], rc_r.at[w, k], core)

    def rs_x(w, k, j):
        return copy(rxs.at[w, k, mto(j)], rxr.at[w, k, j], rx_s.at[w, k, j], rx_r.at[w, k, j], (dp, mto(j)))

    def rs_z(w, k):
        return copy(rzs.at[w, k], rzr.at[w, k], rz_s.at[w, k], rz_r.at[w, k], (2 * zto(k) + c, m))

    def w_part(w, d):
        return dot(xt[w, d], dpre[w], 1, 0)

    def backward(w, grad):
        u = unit[w]
        d = (grad - u * jnp.sum(u * grad, axis=1, keepdims=True)) / rad[w]
        dpre[w] = d.astype(BF16)

        def body(i):
            k = lax.rem(i, nz)
            rcs[w, k] = w_part(w, 2 * zto(k) + other).astype(BF16)
            rs_core(w, k).start()

        loop(1, nz + 1, body)

    def to_mp(w):
        def body(i):
            k = lax.rem(i, nz)
            rs_core(w, k).wait_recv()
            fs[:big, :] = w_part(w, 2 * zto(k) + c) + rcr[w, k].astype(F32)
            for q in range(nm):
                rxs[w, k, q] = fs[q * wrows:(q + 1) * wrows, :].astype(BF16)
            for j in range(1, nm):
                rs_x(w, k, j).start()

        loop(1, nz + 1, body)

    def to_z(w):
        def body(i):
            k = lax.rem(i, nz)
            total = rxs[w, k, m].astype(F32)
            for j in range(1, nm):
                rs_x(w, k, j).wait_recv()
                total = total + rxr[w, k, j].astype(F32)

            @pl.when(k > 0)
            def _():
                rzs[w, k] = total.astype(BF16)
                rs_z(w, k).start()

            @pl.when(k == 0)
            def _():
                rown[w] = total

        loop(1, nz + 1, body)

    def finish(w, out):
        total = rown[w]
        for k in range(1, nz):
            rs_z(w, k).wait_recv()
            total = total + rzr[w, k].astype(F32)
        out[...] = total

    grad = gown[IMG]
    for j in range(1, nm):
        grad_img(j).wait_recv()
        grad = grad + dir_[j].astype(F32)
    backward(IMG, sim * grad)
    gimg[...] = dot(dpre[IMG], wfull[IMG], 1, 1).astype(BF16)
    to_mp(IMG)
    grad = gown[TXT]
    for k in range(1, nz):
        grad_z(k).wait_recv()
        grad = grad + tzr[k].astype(F32)
    backward(TXT, sim * grad)
    to_mp(TXT)
    to_z(IMG)
    gtxt[...] = dot(dpre[TXT], wfull[TXT], 1, 1).astype(BF16)
    to_z(TXT)
    finish(IMG, dwimg)
    finish(TXT, dwtxt)

    for k in range(nz):
        ids_core(k).wait_send()
        txt_c(k).wait_send()
        grad_core(k).wait_send()
        if k > 0:
            ids_txt(k).wait_send()
            txt_z(k).wait_send()
            grad_z(k).wait_send()
    for j in range(1, nm):
        ids_img(j).wait_send()
        img_x(j).wait_send()
        grad_img(j).wait_send()
    for w in (TXT, IMG):
        def body(k):
            for j in range(nm):
                w_c(w, k, j).wait_send()
            rs_core(w, k).wait_send()
            for j in range(1, nm):
                w_x(w, k, j).wait_send()
                rs_x(w, k, j).wait_send()

            @pl.when(k > 0)
            def _():
                w_z(w, k).wait_send()
                rs_z(w, k).wait_send()

        loop(0, nz, body)


def call(nz, nm, args):
    ximg, xtxt, wimg, wtxt, idimg, idtxt, sim, off = args
    rows, depth = ximg.shape
    wrows, width = wimg.shape
    big = nm * wrows
    ndp = 2 * nz
    dma = pltpu.SemaphoreType.DMA
    vm = pltpu.VMEM
    sems = [
        dma((2, nz)), dma((2, nz)), dma((2, nz, nm)), dma((2, nz, nm)), dma((2, nz, nm)), dma((2, nz, nm)),
        dma((nm,)), dma((nm,)), dma((nz,)), dma((nz,)), dma((nz,)), dma((nz,)),
        dma((nm,)), dma((nm,)), dma((nz,)), dma((nz,)), dma((nz,)), dma((nz,)),
        dma((nz,)), dma((nz,)), dma((nz,)), dma((nz,)), dma((nm,)), dma((nm,)),
        dma((2, nz)), dma((2, nz)), dma((2, nz, nm)), dma((2, nz, nm)), dma((2, nz)), dma((2, nz)),
    ]
    scratch = [
        vm((2, ndp, nm, wrows, width), BF16),
        vm((2, depth, width), BF16),
        vm((math.lcm(big, 16), width), F32),
        vm((2, ndp, big, rows), BF16),
        vm((2, rows, width), F32),
        vm((2, rows, 1), F32),
        vm((2, rows, width), BF16),
        vm((nm * rows, width), BF16),
        vm((ndp * rows, width), BF16),
        vm((nm, 8, rows), jnp.int32),
        vm((ndp, 8, rows), jnp.int32),
        vm((nm * rows, ndp * rows), BF16),
        vm((2, rows, width), F32),
        vm((nz, rows, width), BF16),
        vm((nz, rows, width), BF16),
        vm((nz, rows, width), BF16),
        vm((nz, rows, width), BF16),
        vm((nm, rows, width), BF16),
        vm((nm, rows, width), BF16),
        vm((2, rows, width), F32),
        vm((2, nz, big, width), BF16),
        vm((2, nz, big, width), BF16),
        vm((2, nz, nm, wrows, width), BF16),
        vm((2, nz, nm, wrows, width), BF16),
        vm((2, nz, wrows, width), BF16),
        vm((2, nz, wrows, width), BF16),
        vm((2, wrows, width), F32),
    ]
    whole = pl.BlockSpec(memory_space=pltpu.VMEM)
    scalar = pl.BlockSpec(memory_space=pltpu.SMEM)
    return pl.pallas_call(
        functools.partial(kernel, nz, nm, rows, wrows),
        out_shape=(
            jax.ShapeDtypeStruct((rows, depth), BF16),
            jax.ShapeDtypeStruct((rows, depth), BF16),
            jax.ShapeDtypeStruct((wrows, width), F32),
            jax.ShapeDtypeStruct((wrows, width), F32),
        ),
        in_specs=[whole] * 6 + [scalar] * 2,
        out_specs=(whole,) * 4,
        scratch_shapes=scratch + sems,
        compiler_params=pltpu.CompilerParams(
            collective_id=0, has_side_effects=True, vmem_limit_bytes=62 * 1024 * 1024
        ),
        cost_estimate=pl.CostEstimate(flops=6 * 10**9, bytes_accessed=4 * 10**6, transcendentals=0),
    )(
        ximg, xtxt, wimg, wtxt,
        jnp.broadcast_to(idimg[None, :], (8, rows)), jnp.broadcast_to(idtxt[None, :], (8, rows)),
        sim, off,
    )


def solution(mesh):
    ndp, nm = mesh.shape["dp"], mesh.shape["mp"]

    def on_device(*args):
        return call(ndp // 2, nm, args)

    spec = P(("dp", "mp"), None)
    ids = P(("dp", "mp"))
    return jax.shard_map(
        on_device,
        mesh=mesh,
        in_specs=(spec, spec, spec, spec, ids, ids, P(), P()),
        out_specs=(spec,) * 4,
        check_vma=False,
    )
```

```python
import functools
import math

import jax
import jax.numpy as jnp
from jax import lax
from jax.experimental import pallas as pl
from jax.experimental.pallas import tpu as pltpu
from jax.sharding import PartitionSpec as P

MESH = pl.DeviceIdType.MESH
TXT, IMG = 0, 1
F32, BF16 = jnp.float32, jnp.bfloat16


def dot(a, b, da, db):
    return lax.dot_general(a, b, (((da,), (db,)), ((), ())), preferred_element_type=F32)


def loop(low, high, body):
    def step(i, carry):
        body(i)
        return carry

    lax.fori_loop(low, high, step, 0)


def kernel(
    nz, nm, rows, wrows,
    ximg, xtxt, wimg, wtxt, idimg, idtxt, sim_ref, off_ref,
    gimg, gtxt, dwimg, dwtxt,
    wbuf, wfull, fs, xt, unit, rad, dpre, imgs, txts, iids, tids, slopes,
    dt, tcs, tcr, tzs, tzr, dis, dir_, gown,
    rcs, rcr, rxs, rxr, rys, ryr, rzs, rzr, rown,
    wz_s, wz_r, wx_s, wx_r, wc_s, wc_r,
    ii_s, ii_r, ti_s, ti_r, tj_s, tj_r,
    im_s, im_r, tx_s, tx_r, ty_s, ty_r,
    tc_s, tc_r, tz_s, tz_r, di_s, di_r,
    rc_s, rc_r, rx_s, rx_r, rz_s, rz_r,
):
    dp, m = lax.axis_index("dp"), lax.axis_index("mp")
    z, c = lax.div(dp, 2), lax.rem(dp, 2)
    other = 1 - c
    big = nm * wrows
    group = fs.shape[0] // big
    x_refs, w_refs = (xtxt, ximg), (wtxt, wimg)

    def zat(k):
        return lax.rem(z - k + nz, nz)

    def zto(k):
        return lax.rem(z + k, nz)

    def mat(k):
        return lax.rem(m - k + nm, nm)

    def mto(k):
        return lax.rem(m + k, nm)

    core = (2 * z + other, m)
    square = nm == 4
    xbit, ybit = lax.rem(m, 2), lax.div(m, 2)
    across = (m, m + 1 - 2 * xbit, m + 2 - 4 * ybit, 3 - m)
    near = (1, 2) if square else range(1, nm)

    def whom(j):
        return across[j] if square else mto(j)

    def whose(j):
        return across[j] if square else mat(j)

    def pick(k, even, odd):
        return even + lax.rem(k, 2) * (odd - even)

    def copy(src, dst, s, r, dev):
        return pltpu.make_async_remote_copy(
            src_ref=src, dst_ref=dst, send_sem=s, recv_sem=r, device_id=dev, device_id_type=MESH
        )

    barrier = pltpu.get_barrier_semaphore()
    for k in range(1, nz):
        pl.semaphore_signal(barrier, inc=1, device_id=(2 * zto(k) + c, m), device_id_type=MESH)
    for k in range(1, nm):
        pl.semaphore_signal(barrier, inc=1, device_id=(dp, mto(k)), device_id_type=MESH)
    pl.semaphore_signal(barrier, inc=1, device_id=core, device_id_type=MESH)
    pl.semaphore_wait(barrier, nz + nm - 1)

    def w_z(w, k):
        return copy(w_refs[w], wbuf.at[w, dp, m], wz_s.at[w, k], wz_r.at[w, k], (2 * zto(k) + c, m))

    def w_x(w, k, j):
        slot = wbuf.at[w, 2 * zat(k) + c, m]
        return copy(slot, slot, wx_s.at[w, k, j], wx_r.at[w, k, j], (dp, whom(j)))

    def w_diag(w, k):
        slot = wbuf.at[w, 2 * zat(k) + c, pick(k, across[1], across[2])]
        return copy(slot, slot, wx_s.at[w, k, 3], wx_r.at[w, k, 3], (dp, pick(k, across[2], across[1])))

    def w_c(w, k, j):
        slot = wbuf.at[w, 2 * zat(k) + c, whose(j)]
        return copy(slot, slot, wc_s.at[w, k, j], wc_r.at[w, k, j], core)

    def w_z_wait(w, k):
        slot = wbuf.at[w, 2 * zat(k) + c, m]
        copy(slot, slot, wz_s.at[w, k], wz_r.at[w, k], core).wait_recv()

    def w_x_wait(w, k, j):
        slot = wbuf.at[w, 2 * zat(k) + c, whose(j)]
        copy(slot, slot, wx_s.at[w, k, j], wx_r.at[w, k, j], core).wait_recv()

    def w_c_wait(w, k, j):
        slot = wbuf.at[w, 2 * zat(k) + other, whose(j)]
        copy(slot, slot, wc_s.at[w, k, j], wc_r.at[w, k, j], core).wait_recv()

    def w_start(w):
        for k in range(1, nz):
            w_z(w, k).start()
        wbuf[w, dp, m] = w_refs[w][...]
        for j in near:
            w_x(w, 0, j).start()
        w_c(w, 0, 0).start()

    def w_pass_z(w):
        def body(k):
            w_z_wait(w, k)
            for j in near:
                w_x(w, k, j).start()
            w_c(w, k, 0).start()

        loop(1, nz, body)

    def w_pass_x(w):
        def body(k):
            for j in near:
                w_x_wait(w, k, j)
                w_c(w, k, j).start()
            if square:
                w_diag(w, k).start()

        loop(0, nz, body)

    def join(w, d):
        for q in range(nm):
            fs[q * wrows:(q + 1) * wrows, :] = wbuf[w, d, q].astype(F32)
        wfull[w, pl.ds(pl.multiple_of(d * big, 16), big), :] = fs[...].astype(BF16)

    def w_finish(w):
        def own(k):
            if square:
                w_x_wait(w, k, 3)
                w_c(w, k, 3).start()
            if group == 1:
                join(w, 2 * zat(k) + c)

        loop(0, nz, own)

        def rest(k):
            for j in range(nm):
                w_c_wait(w, k, j)
            if group == 1:
                join(w, 2 * zat(k) + other)

        loop(0, nz, rest)

        def join_group(g):
            for n in range(group * nm):
                d = g * group + n // nm
                fs[n * wrows:(n + 1) * wrows, :] = wbuf[w, d, n % nm].astype(F32)
            wfull[w, pl.ds(pl.multiple_of(g * group * big, 16), group * big), :] = fs[...].astype(BF16)

        if group > 1:
            loop(0, 2 * nz // group, join_group)

    def embed(w):
        pre = dot(x_refs[w][...], wfull[w], 1, 0)
        radius = jnp.sqrt(jnp.sum(pre * pre, axis=1, keepdims=True) + 1e-06)
        out = pre / radius
        unit[w] = out
        rad[w] = radius
        return out.astype(BF16)

    def my(n):
        return pl.ds(pl.multiple_of(n * rows, rows), rows)

    def ids_img(j):
        return copy(iids.at[m], iids.at[m], ii_s.at[j], ii_r.at[j], (dp, mto(j)))

    def ids_txt(k):
        return copy(tids.at[dp], tids.at[dp], ti_s.at[k], ti_r.at[k], (2 * zto(k) + c, m))

    def ids_core(k):
        slot = tids.at[2 * zat(k) + c]
        return copy(slot, slot, tj_s.at[k], tj_r.at[k], core)

    def img_x(j):
        slot = imgs.at[my(m), :]
        return copy(slot, slot, im_s.at[j], im_r.at[j], (dp, mto(j)))

    def txt_z(k):
        slot = txts.at[my(dp), :]
        return copy(slot, slot, tx_s.at[k], tx_r.at[k], (2 * zto(k) + c, m))

    def txt_c(k):
        slot = txts.at[my(2 * zat(k) + c), :]
        return copy(slot, slot, ty_s.at[k], ty_r.at[k], core)

    w_start(IMG)
    iids[m] = jnp.broadcast_to(idimg[...], (8, rows))
    tids[dp] = jnp.broadcast_to(idtxt[...], (8, rows))
    for j in range(1, nm):
        ids_img(j).start()
    for k in range(1, nz):
        ids_txt(k).start()
    ids_core(0).start()
    w_pass_z(IMG)
    w_start(TXT)
    w_pass_x(IMG)
    for k in range(1, nz):
        slot = tids.at[2 * zat(k) + c]
        copy(slot, slot, ti_s.at[k], ti_r.at[k], core).wait_recv()
        ids_core(k).start()
    for w in (TXT, IMG):
        turned = x_refs[w][...].T if group == 1 else x_refs[w][...].astype(F32).T
        for d in range(2 * nz):
            xt[w, d] = turned[d * big:(d + 1) * big, :].astype(BF16)
    w_pass_z(TXT)
    w_finish(IMG)
    imgs[my(m), :] = embed(IMG)
    for j in range(1, nm):
        img_x(j).start()
    w_pass_x(TXT)
    w_finish(TXT)
    txts[my(dp), :] = embed(TXT)
    txt_c(0).start()
    for k in range(1, nz):
        txt_z(k).start()

    for j in range(1, nm):
        slot = iids.at[mat(j)]
        copy(slot, slot, ii_s.at[j], ii_r.at[j], core).wait_recv()
    for k in range(nz):
        slot = tids.at[2 * zat(k) + other]
        copy(slot, slot, tj_s.at[k], tj_r.at[k], core).wait_recv()
    for j in range(1, nm):
        slot = imgs.at[my(mat(j)), :]
        copy(slot, slot, im_s.at[j], im_r.at[j], core).wait_recv()

    sim, off = sim_ref[0], off_ref[0]

    def grad_core(k):
        return copy(tcs.at[k], tcr.at[k], tc_s.at[k], tc_r.at[k], core)

    def grad_z(k):
        return copy(tzs.at[k], tzr.at[k], tz_s.at[k], tz_r.at[k], (2 * zat(k) + c, m))

    def pair(k):
        zs = zat(k)

        @pl.when(k > 0)
        def _():
            slot = txts.at[my(2 * zs + c), :]
            copy(slot, slot, tx_s.at[k], tx_r.at[k], core).wait_recv()
            txt_c(k).start()

        slot = txts.at[my(2 * zs + other), :]
        copy(slot, slot, ty_s.at[k], ty_r.at[k], core).wait_recv()
        span = pl.ds(pl.multiple_of(zs * 2 * rows, 2 * rows), 2 * rows)
        idrow = jnp.concatenate([tids[2 * zs][:1], tids[2 * zs + 1][:1]], axis=1)

        logits = sim * dot(imgs[...], txts[span, :], 1, 1) + off
        idcol = jnp.concatenate([iids[q].T[:, :1] for q in range(nm)], axis=0)
        sign = jnp.where(idcol == idrow, 1.0, -1.0).astype(F32)
        slope = (-sign * jax.nn.sigmoid(-sign * logits)).astype(BF16)
        slopes[:, span] = slope
        part = dot(slope, imgs[...], 0, 0)
        for h in range(2):
            dt[h] = part[h * rows:(h + 1) * rows, :]
        tcs[k] = dt[other].astype(BF16)
        grad_core(k).start()
        grad_core(k).wait_recv()

        @pl.when(k > 0)
        def _():
            tzs[k] = (dt[c] + tcr[k].astype(F32)).astype(BF16)
            grad_z(k).start()

        @pl.when(k == 0)
        def _():
            gown[TXT] = dt[c] + tcr[k].astype(F32)

    loop(0, nz, pair)

    def grad_img(j):
        return copy(dis.at[j], dir_.at[j], di_s.at[j], di_r.at[j], (dp, mto(j)))

    def img_part(j):
        part = dot(slopes[my(mto(j)), :], txts[...], 1, 0)

        @pl.when(j < nm)
        def _():
            dis[j] = part.astype(BF16)
            grad_img(j).start()

        @pl.when(j == nm)
        def _():
            gown[IMG] = part

    loop(1, nm + 1, img_part)

    def rs_core(w, k):
        return copy(rcs.at[w, k], rcr.at[w, k], rc_s.at[w, k], rc_r.at[w, k], core)

    def rs_x(w, k):
        there = (dp, pick(k, across[1], across[2]))
        return copy(rxs.at[w, k, pl.ds(2, 2)], rxr.at[w, k], rx_s.at[w, k, 0], rx_r.at[w, k, 0], there)

    def rs_far(w, k, j):
        return copy(rxs.at[w, k, mto(j)], rxr.at[w, k, j], rx_s.at[w, k, j], rx_r.at[w, k, j], (dp, mto(j)))

    def rs_y(w, k):
        there = (dp, pick(k, across[2], across[1]))
        return copy(rys.at[w, k], ryr.at[w, k], rx_s.at[w, k, 1], rx_r.at[w, k, 1], there)

    def rs_z(w, k):
        return copy(rzs.at[w, k], rzr.at[w, k], rz_s.at[w, k], rz_r.at[w, k], (2 * zto(k) + c, m))

    def w_part(w, d):
        return dot(xt[w, d], dpre[w], 1, 0)

    def backward(w, grad):
        u = unit[w]
        d = (grad - u * jnp.sum(u * grad, axis=1, keepdims=True)) / rad[w]
        dpre[w] = d.astype(BF16)

        def body(i):
            k = lax.rem(i, nz)
            rcs[w, k] = w_part(w, 2 * zto(k) + other).astype(BF16)
            rs_core(w, k).start()

        loop(1, nz + 1, body)

    def to_mp(w):
        def body(i):
            k = lax.rem(i, nz)
            rs_core(w, k).wait_recv()
            fs[:big, :] = w_part(w, 2 * zto(k) + c) + rcr[w, k].astype(F32)
            for q in range(nm):
                dx, dy = lax.rem(xbit + q % 2, 2), lax.rem(ybit + q // 2, 2)
                place = pick(k, 2 * dx + dy, 2 * dy + dx) if square else q
                rxs[w, k, place] = fs[q * wrows:(q + 1) * wrows, :].astype(BF16)
            if square:
                rs_x(w, k).start()
            else:
                for j in near:
                    rs_far(w, k, j).start()

        loop(1, nz + 1, body)

    def to_y(w):
        def body(i):
            k = lax.rem(i, nz)
            rs_x(w, k).wait_recv()
            rys[w, k] = (rxs[w, k, 1].astype(F32) + rxr[w, k, 1].astype(F32)).astype(BF16)
            rs_y(w, k).start()

        if square:
            loop(1, nz + 1, body)

    def to_z(w):
        def body(i):
            k = lax.rem(i, nz)
            if square:
                rs_y(w, k).wait_recv()
                total = rxs[w, k, 0].astype(F32) + rxr[w, k, 0].astype(F32) + ryr[w, k].astype(F32)
            else:
                total = rxs[w, k, m].astype(F32)
                for j in near:
                    rs_far(w, k, j).wait_recv()
                    total = total + rxr[w, k, j].astype(F32)

            @pl.when(k > 0)
            def _():
                rzs[w, k] = total.astype(BF16)
                rs_z(w, k).start()

            @pl.when(k == 0)
            def _():
                rown[w] = total

        loop(1, nz + 1, body)

    def finish(w, out):
        total = rown[w]
        for k in range(1, nz):
            rs_z(w, k).wait_recv()
            total = total + rzr[w, k].astype(F32)
        out[...] = total

    grad = gown[IMG]
    for j in range(1, nm):
        grad_img(j).wait_recv()
        grad = grad + dir_[j].astype(F32)
    backward(IMG, sim * grad)
    gimg[...] = dot(dpre[IMG], wfull[IMG], 1, 1).astype(BF16)
    to_mp(IMG)
    to_y(IMG)
    grad = gown[TXT]
    for k in range(1, nz):
        grad_z(k).wait_recv()
        grad = grad + tzr[k].astype(F32)
    backward(TXT, sim * grad)
    to_mp(TXT)
    to_z(IMG)
    to_y(TXT)
    gtxt[...] = dot(dpre[TXT], wfull[TXT], 1, 1).astype(BF16)
    to_z(TXT)
    finish(IMG, dwimg)
    finish(TXT, dwtxt)

    for k in range(nz):
        ids_core(k).wait_send()
        txt_c(k).wait_send()
        grad_core(k).wait_send()
        if k > 0:
            ids_txt(k).wait_send()
            txt_z(k).wait_send()
            grad_z(k).wait_send()
    for j in range(1, nm):
        ids_img(j).wait_send()
        img_x(j).wait_send()
        grad_img(j).wait_send()
    for w in (TXT, IMG):
        def body(k):
            for j in range(nm):
                w_c(w, k, j).wait_send()
            rs_core(w, k).wait_send()
            for j in near:
                w_x(w, k, j).wait_send()
            if square:
                w_diag(w, k).wait_send()
                rs_x(w, k).wait_send()
                rs_y(w, k).wait_send()
            else:
                for j in near:
                    rs_far(w, k, j).wait_send()

            @pl.when(k > 0)
            def _():
                w_z(w, k).wait_send()
                rs_z(w, k).wait_send()

        loop(0, nz, body)


def call(nz, nm, args):
    ximg, xtxt, wimg, wtxt, idimg, idtxt, sim, off = args
    rows, depth = ximg.shape
    wrows, width = wimg.shape
    big = nm * wrows
    ndp = 2 * nz
    dma = pltpu.SemaphoreType.DMA
    vm = pltpu.VMEM
    sems = [
        dma((2, nz)), dma((2, nz)), dma((2, nz, nm)), dma((2, nz, nm)), dma((2, nz, nm)), dma((2, nz, nm)),
        dma((nm,)), dma((nm,)), dma((nz,)), dma((nz,)), dma((nz,)), dma((nz,)),
        dma((nm,)), dma((nm,)), dma((nz,)), dma((nz,)), dma((nz,)), dma((nz,)),
        dma((nz,)), dma((nz,)), dma((nz,)), dma((nz,)), dma((nm,)), dma((nm,)),
        dma((2, nz)), dma((2, nz)), dma((2, nz, nm)), dma((2, nz, nm)), dma((2, nz)), dma((2, nz)),
    ]
    scratch = [
        vm((2, ndp, nm, wrows, width), BF16),
        vm((2, depth, width), BF16),
        vm((math.lcm(big, 16), width), F32),
        vm((2, ndp, big, rows), BF16),
        vm((2, rows, width), F32),
        vm((2, rows, 1), F32),
        vm((2, rows, width), BF16),
        vm((nm * rows, width), BF16),
        vm((ndp * rows, width), BF16),
        vm((nm, 8, rows), jnp.int32),
        vm((ndp, 8, rows), jnp.int32),
        vm((nm * rows, ndp * rows), BF16),
        vm((2, rows, width), F32),
        vm((nz, rows, width), BF16),
        vm((nz, rows, width), BF16),
        vm((nz, rows, width), BF16),
        vm((nz, rows, width), BF16),
        vm((nm, rows, width), BF16),
        vm((nm, rows, width), BF16),
        vm((2, rows, width), F32),
        vm((2, nz, big, width), BF16),
        vm((2, nz, big, width), BF16),
        vm((2, nz, nm, wrows, width), BF16),
        vm((2, nz, 2 if nm == 4 else nm, wrows, width), BF16),
        vm((2, nz, wrows, width), BF16),
        vm((2, nz, wrows, width), BF16),
        vm((2, nz, wrows, width), BF16),
        vm((2, nz, wrows, width), BF16),
        vm((2, wrows, width), F32),
    ]
    whole = pl.BlockSpec(memory_space=pltpu.VMEM)
    scalar = pl.BlockSpec(memory_space=pltpu.SMEM)
    return pl.pallas_call(
        functools.partial(kernel, nz, nm, rows, wrows),
        out_shape=(
            jax.ShapeDtypeStruct((rows, depth), BF16),
            jax.ShapeDtypeStruct((rows, depth), BF16),
            jax.ShapeDtypeStruct((wrows, width), F32),
            jax.ShapeDtypeStruct((wrows, width), F32),
        ),
        in_specs=[whole] * 6 + [scalar] * 2,
        out_specs=(whole,) * 4,
        scratch_shapes=scratch + sems,
        compiler_params=pltpu.CompilerParams(
            collective_id=0, has_side_effects=True, vmem_limit_bytes=62 * 1024 * 1024
        ),
        cost_estimate=pl.CostEstimate(flops=6 * 10**9, bytes_accessed=4 * 10**6, transcendentals=0),
    )(
        ximg, xtxt, wimg, wtxt,
        idimg[None, :], idtxt[None, :],
        sim, off,
    )


def solution(mesh):
    ndp, nm = mesh.shape["dp"], mesh.shape["mp"]

    def on_device(*args):
        return call(ndp // 2, nm, args)

    spec = P(("dp", "mp"), None)
    ids = P(("dp", "mp"))
    return jax.shard_map(
        on_device,
        mesh=mesh,
        in_specs=(spec, spec, spec, spec, ids, ids, P(), P()),
        out_specs=(spec,) * 4,
        check_vma=False,
    )
```

```python
import functools
import math

import jax
import jax.numpy as jnp
from jax import lax
from jax.experimental import pallas as pl
from jax.experimental.pallas import tpu as pltpu
from jax.sharding import PartitionSpec as P

MESH = pl.DeviceIdType.MESH
TXT, IMG = 0, 1
F32, BF16 = jnp.float32, jnp.bfloat16


def dot(a, b, da, db):
    return lax.dot_general(a, b, (((da,), (db,)), ((), ())), preferred_element_type=F32)


def loop(low, high, body):
    def step(i, carry):
        body(i)
        return carry

    lax.fori_loop(low, high, step, 0)


def kernel(
    nz, nm, rows, wrows,
    ximg, xtxt, wimg, wtxt, idimg, idtxt, sim_ref, off_ref,
    gimg, gtxt, dwimg, dwtxt,
    wbuf, wfull, fs, xt, unit, rad, dpre, imgs, txts, iids, tids, slopes,
    dt, tcs, tcr, tzs, tzr, dis, dir_, gown,
    rcs, rcr, rxs, rxr, rys, ryr, rzs, rzr, rown,
    wz_s, wz_r, wx_s, wx_r, wc_s, wc_r,
    ii_s, ii_r, ti_s, ti_r, tj_s, tj_r,
    im_s, im_r, tx_s, tx_r, ty_s, ty_r,
    tc_s, tc_r, tz_s, tz_r, di_s, di_r,
    rc_s, rc_r, rx_s, rx_r, rz_s, rz_r,
):
    dp, m = lax.axis_index("dp"), lax.axis_index("mp")
    z, c = lax.div(dp, 2), lax.rem(dp, 2)
    other = 1 - c
    big = nm * wrows
    group = fs.shape[0] // big
    x_refs, w_refs = (xtxt, ximg), (wtxt, wimg)

    def zat(k):
        return lax.rem(z - k + nz, nz)

    def zto(k):
        return lax.rem(z + k, nz)

    def mat(k):
        return lax.rem(m - k + nm, nm)

    def mto(k):
        return lax.rem(m + k, nm)

    core = (2 * z + other, m)
    square = nm == 4
    xbit, ybit = lax.rem(m, 2), lax.div(m, 2)
    across = (m, m + 1 - 2 * xbit, m + 2 - 4 * ybit, 3 - m)
    near = (1, 2) if square else range(1, nm)

    def whom(j):
        return across[j] if square else mto(j)

    def whose(j):
        return across[j] if square else mat(j)

    def pick(k, even, odd):
        return even + lax.rem(k, 2) * (odd - even)

    def copy(src, dst, s, r, dev):
        return pltpu.make_async_remote_copy(
            src_ref=src, dst_ref=dst, send_sem=s, recv_sem=r, device_id=dev, device_id_type=MESH
        )

    barrier = pltpu.get_barrier_semaphore()
    for k in range(1, nz):
        pl.semaphore_signal(barrier, inc=1, device_id=(2 * zto(k) + c, m), device_id_type=MESH)
    for k in range(1, nm):
        pl.semaphore_signal(barrier, inc=1, device_id=(dp, mto(k)), device_id_type=MESH)
    pl.semaphore_signal(barrier, inc=1, device_id=core, device_id_type=MESH)
    pl.semaphore_wait(barrier, nz + nm - 1)

    def w_z(w, k):
        return copy(w_refs[w], wbuf.at[w, dp, m], wz_s.at[w, k], wz_r.at[w, k], (2 * zto(k) + c, m))

    def w_x(w, k, j):
        slot = wbuf.at[w, 2 * zat(k) + c, m]
        return copy(slot, slot, wx_s.at[w, k, j], wx_r.at[w, k, j], (dp, whom(j)))

    def w_diag(w, k):
        slot = wbuf.at[w, 2 * zat(k) + c, pick(k, across[1], across[2])]
        return copy(slot, slot, wx_s.at[w, k, 3], wx_r.at[w, k, 3], (dp, pick(k, across[2], across[1])))

    def w_c(w, k, j):
        slot = wbuf.at[w, 2 * zat(k) + c, whose(j)]
        return copy(slot, slot, wc_s.at[w, k, j], wc_r.at[w, k, j], core)

    def w_z_wait(w, k):
        slot = wbuf.at[w, 2 * zat(k) + c, m]
        copy(slot, slot, wz_s.at[w, k], wz_r.at[w, k], core).wait_recv()

    def w_x_wait(w, k, j):
        slot = wbuf.at[w, 2 * zat(k) + c, whose(j)]
        copy(slot, slot, wx_s.at[w, k, j], wx_r.at[w, k, j], core).wait_recv()

    def w_c_wait(w, k, j):
        slot = wbuf.at[w, 2 * zat(k) + other, whose(j)]
        copy(slot, slot, wc_s.at[w, k, j], wc_r.at[w, k, j], core).wait_recv()

    def w_start(w):
        for k in range(1, nz):
            w_z(w, k).start()
        wbuf[w, dp, m] = w_refs[w][...]
        for j in near:
            w_x(w, 0, j).start()
        w_c(w, 0, 0).start()

    def w_pass_z(w):
        def body(k):
            w_z_wait(w, k)
            for j in near:
                w_x(w, k, j).start()
            w_c(w, k, 0).start()

        loop(1, nz, body)

    def w_pass_x(w):
        def body(k):
            for j in near:
                w_x_wait(w, k, j)
                w_c(w, k, j).start()
            if square:
                w_diag(w, k).start()

        loop(0, nz, body)

    def join(w, d):
        for q in range(nm):
            fs[q * wrows:(q + 1) * wrows, :] = wbuf[w, d, q].astype(F32)
        wfull[w, pl.ds(pl.multiple_of(d * big, 16), big), :] = fs[...].astype(BF16)

    def w_finish(w):
        def own(k):
            if square:
                w_x_wait(w, k, 3)
                w_c(w, k, 3).start()
            if group == 1:
                join(w, 2 * zat(k) + c)

        loop(0, nz, own)

        def rest(k):
            for j in range(nm):
                w_c_wait(w, k, j)
            if group == 1:
                join(w, 2 * zat(k) + other)

        loop(0, nz, rest)

        def join_group(g):
            for n in range(group * nm):
                d = g * group + n // nm
                fs[n * wrows:(n + 1) * wrows, :] = wbuf[w, d, n % nm].astype(F32)
            wfull[w, pl.ds(pl.multiple_of(g * group * big, 16), group * big), :] = fs[...].astype(BF16)

        if group > 1:
            loop(0, 2 * nz // group, join_group)

    def embed(w):
        pre = dot(x_refs[w][...], wfull[w], 1, 0)
        radius = jnp.sqrt(jnp.sum(pre * pre, axis=1, keepdims=True) + 1e-06)
        out = pre / radius
        unit[w] = out
        rad[w] = radius
        return out.astype(BF16)

    def my(n):
        return pl.ds(pl.multiple_of(n * rows, rows), rows)

    def ids_img(j):
        return copy(iids.at[m], iids.at[m], ii_s.at[j], ii_r.at[j], (dp, mto(j)))

    def ids_txt(k):
        return copy(tids.at[dp], tids.at[dp], ti_s.at[k], ti_r.at[k], (2 * zto(k) + c, m))

    def ids_core(k):
        slot = tids.at[2 * zat(k) + c]
        return copy(slot, slot, tj_s.at[k], tj_r.at[k], core)

    def img_x(j):
        slot = imgs.at[my(m), :]
        return copy(slot, slot, im_s.at[j], im_r.at[j], (dp, mto(j)))

    def txt_z(k):
        slot = txts.at[my(dp), :]
        return copy(slot, slot, tx_s.at[k], tx_r.at[k], (2 * zto(k) + c, m))

    def txt_c(k):
        slot = txts.at[my(2 * zat(k) + c), :]
        return copy(slot, slot, ty_s.at[k], ty_r.at[k], core)

    w_start(TXT)
    iids[m] = jnp.broadcast_to(idimg[...], (8, rows))
    tids[dp] = jnp.broadcast_to(idtxt[...], (8, rows))
    for j in range(1, nm):
        ids_img(j).start()
    for k in range(1, nz):
        ids_txt(k).start()
    ids_core(0).start()
    w_pass_z(TXT)
    w_start(IMG)
    w_pass_x(TXT)
    for k in range(1, nz):
        slot = tids.at[2 * zat(k) + c]
        copy(slot, slot, ti_s.at[k], ti_r.at[k], core).wait_recv()
        ids_core(k).start()
    for w in (TXT, IMG):
        turned = x_refs[w][...].T if group == 1 else x_refs[w][...].astype(F32).T
        for d in range(2 * nz):
            xt[w, d] = turned[d * big:(d + 1) * big, :].astype(BF16)
    w_pass_z(IMG)
    w_finish(TXT)
    txts[my(dp), :] = embed(TXT)
    for k in range(1, nz):
        txt_z(k).start()
    txt_c(0).start()
    w_pass_x(IMG)
    w_finish(IMG)
    imgs[my(m), :] = embed(IMG)
    for j in range(1, nm):
        img_x(j).start()

    def take_txt(k):
        slot = txts.at[my(2 * zat(k) + c), :]
        copy(slot, slot, tx_s.at[k], tx_r.at[k], core).wait_recv()
        txt_c(k).start()

    loop(1, nz, take_txt)
    for j in range(1, nm):
        slot = iids.at[mat(j)]
        copy(slot, slot, ii_s.at[j], ii_r.at[j], core).wait_recv()
    for k in range(nz):
        slot = tids.at[2 * zat(k) + other]
        copy(slot, slot, tj_s.at[k], tj_r.at[k], core).wait_recv()
    for j in range(1, nm):
        slot = imgs.at[my(mat(j)), :]
        copy(slot, slot, im_s.at[j], im_r.at[j], core).wait_recv()

    sim, off = sim_ref[0], off_ref[0]

    def grad_core(k):
        return copy(tcs.at[k], tcr.at[k], tc_s.at[k], tc_r.at[k], core)

    def grad_z(k):
        return copy(tzs.at[k], tzr.at[k], tz_s.at[k], tz_r.at[k], (2 * zat(k) + c, m))

    def pair(i):
        k = lax.rem(i, nz)
        zs = zat(k)

        slot = txts.at[my(2 * zs + other), :]
        copy(slot, slot, ty_s.at[k], ty_r.at[k], core).wait_recv()
        span = pl.ds(pl.multiple_of(zs * 2 * rows, 2 * rows), 2 * rows)
        idrow = jnp.concatenate([tids[2 * zs][:1], tids[2 * zs + 1][:1]], axis=1)

        logits = sim * dot(imgs[...], txts[span, :], 1, 1) + off
        idcol = jnp.concatenate([iids[q].T[:, :1] for q in range(nm)], axis=0)
        sign = jnp.where(idcol == idrow, 1.0, -1.0).astype(F32)
        slope = (-sign * jax.nn.sigmoid(-sign * logits)).astype(BF16)
        slopes[:, span] = slope
        part = dot(slope, imgs[...], 0, 0)
        for h in range(2):
            dt[h] = part[h * rows:(h + 1) * rows, :]
        tcs[k] = dt[other].astype(BF16)
        grad_core(k).start()
        grad_core(k).wait_recv()

        @pl.when(k > 0)
        def _():
            tzs[k] = (dt[c] + tcr[k].astype(F32)).astype(BF16)
            grad_z(k).start()

        @pl.when(k == 0)
        def _():
            gown[TXT] = dt[c] + tcr[k].astype(F32)

    loop(1, nz + 1, pair)

    def grad_img(j):
        return copy(dis.at[j], dir_.at[j], di_s.at[j], di_r.at[j], (dp, mto(j)))

    def img_part(j):
        part = dot(slopes[my(mto(j)), :], txts[...], 1, 0)

        @pl.when(j < nm)
        def _():
            dis[j] = part.astype(BF16)
            grad_img(j).start()

        @pl.when(j == nm)
        def _():
            gown[IMG] = part

    loop(1, nm + 1, img_part)

    def rs_core(w, k):
        return copy(rcs.at[w, k], rcr.at[w, k], rc_s.at[w, k], rc_r.at[w, k], core)

    def rs_x(w, k):
        there = (dp, pick(k, across[1], across[2]))
        return copy(rxs.at[w, k, pl.ds(2, 2)], rxr.at[w, k], rx_s.at[w, k, 0], rx_r.at[w, k, 0], there)

    def rs_far(w, k, j):
        return copy(rxs.at[w, k, mto(j)], rxr.at[w, k, j], rx_s.at[w, k, j], rx_r.at[w, k, j], (dp, mto(j)))

    def rs_y(w, k):
        there = (dp, pick(k, across[2], across[1]))
        return copy(rys.at[w, k], ryr.at[w, k], rx_s.at[w, k, 1], rx_r.at[w, k, 1], there)

    def rs_z(w, k):
        return copy(rzs.at[w, k], rzr.at[w, k], rz_s.at[w, k], rz_r.at[w, k], (2 * zto(k) + c, m))

    def w_part(w, d):
        return dot(xt[w, d], dpre[w], 1, 0)

    def backward(w, grad):
        u = unit[w]
        d = (grad - u * jnp.sum(u * grad, axis=1, keepdims=True)) / rad[w]
        dpre[w] = d.astype(BF16)

        def body(i):
            k = lax.rem(i, nz)
            rcs[w, k] = w_part(w, 2 * zto(k) + other).astype(BF16)
            rs_core(w, k).start()

        loop(1, nz + 1, body)

    def to_mp(w):
        def body(i):
            k = lax.rem(i, nz)
            rs_core(w, k).wait_recv()
            fs[:big, :] = w_part(w, 2 * zto(k) + c) + rcr[w, k].astype(F32)
            for q in range(nm):
                dx, dy = lax.rem(xbit + q % 2, 2), lax.rem(ybit + q // 2, 2)
                place = pick(k, 2 * dx + dy, 2 * dy + dx) if square else q
                rxs[w, k, place] = fs[q * wrows:(q + 1) * wrows, :].astype(BF16)
            if square:
                rs_x(w, k).start()
            else:
                for j in near:
                    rs_far(w, k, j).start()

        loop(1, nz + 1, body)

    def to_y(w):
        def body(i):
            k = lax.rem(i, nz)
            rs_x(w, k).wait_recv()
            rys[w, k] = (rxs[w, k, 1].astype(F32) + rxr[w, k, 1].astype(F32)).astype(BF16)
            rs_y(w, k).start()

        if square:
            loop(1, nz + 1, body)

    def to_z(w):
        def body(i):
            k = lax.rem(i, nz)
            if square:
                rs_y(w, k).wait_recv()
                total = rxs[w, k, 0].astype(F32) + rxr[w, k, 0].astype(F32) + ryr[w, k].astype(F32)
            else:
                total = rxs[w, k, m].astype(F32)
                for j in near:
                    rs_far(w, k, j).wait_recv()
                    total = total + rxr[w, k, j].astype(F32)

            @pl.when(k > 0)
            def _():
                rzs[w, k] = total.astype(BF16)
                rs_z(w, k).start()

            @pl.when(k == 0)
            def _():
                rown[w] = total

        loop(1, nz + 1, body)

    def finish(w, out):
        total = rown[w]
        for k in range(1, nz):
            rs_z(w, k).wait_recv()
            total = total + rzr[w, k].astype(F32)
        out[...] = total

    grad = gown[IMG]
    for j in range(1, nm):
        grad_img(j).wait_recv()
        grad = grad + dir_[j].astype(F32)
    backward(IMG, sim * grad)
    gimg[...] = dot(dpre[IMG], wfull[IMG], 1, 1).astype(BF16)
    to_mp(IMG)
    to_y(IMG)
    grad = gown[TXT]
    for k in range(1, nz):
        grad_z(k).wait_recv()
        grad = grad + tzr[k].astype(F32)
    backward(TXT, sim * grad)
    to_mp(TXT)
    to_z(IMG)
    to_y(TXT)
    gtxt[...] = dot(dpre[TXT], wfull[TXT], 1, 1).astype(BF16)
    to_z(TXT)
    finish(IMG, dwimg)
    finish(TXT, dwtxt)

    for k in range(nz):
        ids_core(k).wait_send()
        txt_c(k).wait_send()
        grad_core(k).wait_send()
        if k > 0:
            ids_txt(k).wait_send()
            txt_z(k).wait_send()
            grad_z(k).wait_send()
    for j in range(1, nm):
        ids_img(j).wait_send()
        img_x(j).wait_send()
        grad_img(j).wait_send()
    for w in (TXT, IMG):
        def body(k):
            for j in range(nm):
                w_c(w, k, j).wait_send()
            rs_core(w, k).wait_send()
            for j in near:
                w_x(w, k, j).wait_send()
            if square:
                w_diag(w, k).wait_send()
                rs_x(w, k).wait_send()
                rs_y(w, k).wait_send()
            else:
                for j in near:
                    rs_far(w, k, j).wait_send()

            @pl.when(k > 0)
            def _():
                w_z(w, k).wait_send()
                rs_z(w, k).wait_send()

        loop(0, nz, body)


def call(nz, nm, args):
    ximg, xtxt, wimg, wtxt, idimg, idtxt, sim, off = args
    rows, depth = ximg.shape
    wrows, width = wimg.shape
    big = nm * wrows
    ndp = 2 * nz
    dma = pltpu.SemaphoreType.DMA
    vm = pltpu.VMEM
    sems = [
        dma((2, nz)), dma((2, nz)), dma((2, nz, nm)), dma((2, nz, nm)), dma((2, nz, nm)), dma((2, nz, nm)),
        dma((nm,)), dma((nm,)), dma((nz,)), dma((nz,)), dma((nz,)), dma((nz,)),
        dma((nm,)), dma((nm,)), dma((nz,)), dma((nz,)), dma((nz,)), dma((nz,)),
        dma((nz,)), dma((nz,)), dma((nz,)), dma((nz,)), dma((nm,)), dma((nm,)),
        dma((2, nz)), dma((2, nz)), dma((2, nz, nm)), dma((2, nz, nm)), dma((2, nz)), dma((2, nz)),
    ]
    scratch = [
        vm((2, ndp, nm, wrows, width), BF16),
        vm((2, depth, width), BF16),
        vm((math.lcm(big, 16), width), F32),
        vm((2, ndp, big, rows), BF16),
        vm((2, rows, width), F32),
        vm((2, rows, 1), F32),
        vm((2, rows, width), BF16),
        vm((nm * rows, width), BF16),
        vm((ndp * rows, width), BF16),
        vm((nm, 8, rows), jnp.int32),
        vm((ndp, 8, rows), jnp.int32),
        vm((nm * rows, ndp * rows), BF16),
        vm((2, rows, width), F32),
        vm((nz, rows, width), BF16),
        vm((nz, rows, width), BF16),
        vm((nz, rows, width), BF16),
        vm((nz, rows, width), BF16),
        vm((nm, rows, width), BF16),
        vm((nm, rows, width), BF16),
        vm((2, rows, width), F32),
        vm((2, nz, big, width), BF16),
        vm((2, nz, big, width), BF16),
        vm((2, nz, nm, wrows, width), BF16),
        vm((2, nz, 2 if nm == 4 else nm, wrows, width), BF16),
        vm((2, nz, wrows, width), BF16),
        vm((2, nz, wrows, width), BF16),
        vm((2, nz, wrows, width), BF16),
        vm((2, nz, wrows, width), BF16),
        vm((2, wrows, width), F32),
    ]
    whole = pl.BlockSpec(memory_space=pltpu.VMEM)
    scalar = pl.BlockSpec(memory_space=pltpu.SMEM)
    return pl.pallas_call(
        functools.partial(kernel, nz, nm, rows, wrows),
        out_shape=(
            jax.ShapeDtypeStruct((rows, depth), BF16),
            jax.ShapeDtypeStruct((rows, depth), BF16),
            jax.ShapeDtypeStruct((wrows, width), F32),
            jax.ShapeDtypeStruct((wrows, width), F32),
        ),
        in_specs=[whole] * 6 + [scalar] * 2,
        out_specs=(whole,) * 4,
        scratch_shapes=scratch + sems,
        compiler_params=pltpu.CompilerParams(
            collective_id=0, has_side_effects=True, vmem_limit_bytes=62 * 1024 * 1024
        ),
        cost_estimate=pl.CostEstimate(flops=6 * 10**9, bytes_accessed=4 * 10**6, transcendentals=0),
    )(
        ximg, xtxt, wimg, wtxt,
        idimg[None, :], idtxt[None, :],
        sim, off,
    )


def solution(mesh):
    ndp, nm = mesh.shape["dp"], mesh.shape["mp"]

    def on_device(*args):
        return call(ndp // 2, nm, args)

    spec = P(("dp", "mp"), None)
    ids = P(("dp", "mp"))
    return jax.shard_map(
        on_device,
        mesh=mesh,
        in_specs=(spec, spec, spec, spec, ids, ids, P(), P()),
        out_specs=(spec,) * 4,
        check_vma=False,
    )
```

```python
import functools
import math

import jax
import jax.numpy as jnp
from jax import lax
from jax.experimental import pallas as pl
from jax.experimental.pallas import tpu as pltpu
from jax.sharding import PartitionSpec as P

MESH = pl.DeviceIdType.MESH
TXT, IMG = 0, 1
F32, BF16 = jnp.float32, jnp.bfloat16


def dot(a, b, da, db):
    return lax.dot_general(a, b, (((da,), (db,)), ((), ())), preferred_element_type=F32)


def loop(low, high, body):
    def step(i, carry):
        body(i)
        return carry

    lax.fori_loop(low, high, step, 0)


def kernel(
    nz, nm, rows, wrows,
    ximg, xtxt, wimg, wtxt, idimg, idtxt, sim_ref, off_ref,
    gimg, gtxt, dwimg, dwtxt,
    wbuf, wfull, fs, xt, unit, rad, dpre, imgs, txts, iids, tids, slopes,
    dt, tcs, tcr, tzs, tzr, dis, dir_, gown,
    rcs, rcr, rxs, rxr, rys, ryr, rzs, rzr, rown,
    wz_s, wz_r, wx_s, wx_r, wc_s, wc_r,
    ii_s, ii_r, ti_s, ti_r, tj_s, tj_r,
    im_s, im_r, tx_s, tx_r, ty_s, ty_r,
    tc_s, tc_r, tz_s, tz_r, di_s, di_r,
    rc_s, rc_r, rx_s, rx_r, rz_s, rz_r,
):
    dp, m = lax.axis_index("dp"), lax.axis_index("mp")
    z, c = lax.div(dp, 2), lax.rem(dp, 2)
    other = 1 - c
    big = nm * wrows
    group = fs.shape[0] // big
    x_refs, w_refs = (xtxt, ximg), (wtxt, wimg)

    def zat(k):
        return lax.rem(z - k + nz, nz)

    def zto(k):
        return lax.rem(z + k, nz)

    def mat(k):
        return lax.rem(m - k + nm, nm)

    def mto(k):
        return lax.rem(m + k, nm)

    line = nz == 4

    def beyond(k):
        return lax.rem(z + k, 2) + 2 * lax.rem(lax.div(z, 2) + lax.div(k, 2), 2)

    def zof(k):
        return beyond(k) if line else zat(k)

    core = (2 * z + other, m)
    square = nm == 4
    xbit, ybit = lax.rem(m, 2), lax.div(m, 2)
    across = (m, m + 1 - 2 * xbit, m + 2 - 4 * ybit, 3 - m)
    near = (1, 2) if square else range(1, nm)

    def whom(j):
        return across[j] if square else mto(j)

    def whose(j):
        return across[j] if square else mat(j)

    def pick(k, even, odd):
        return even + lax.rem(k, 2) * (odd - even)

    def copy(src, dst, s, r, dev):
        return pltpu.make_async_remote_copy(
            src_ref=src, dst_ref=dst, send_sem=s, recv_sem=r, device_id=dev, device_id_type=MESH
        )

    barrier = pltpu.get_barrier_semaphore()
    for k in range(1, nz):
        pl.semaphore_signal(barrier, inc=1, device_id=(2 * zto(k) + c, m), device_id_type=MESH)
    for k in range(1, nm):
        pl.semaphore_signal(barrier, inc=1, device_id=(dp, mto(k)), device_id_type=MESH)
    pl.semaphore_signal(barrier, inc=1, device_id=core, device_id_type=MESH)
    pl.semaphore_wait(barrier, nz + nm - 1)

    def w_z(w, k):
        return copy(w_refs[w], wbuf.at[w, dp, m], wz_s.at[w, k], wz_r.at[w, k], (2 * zto(k) + c, m))

    def w_x(w, k, j):
        slot = wbuf.at[w, 2 * zat(k) + c, m]
        return copy(slot, slot, wx_s.at[w, k, j], wx_r.at[w, k, j], (dp, whom(j)))

    def w_diag(w, k):
        slot = wbuf.at[w, 2 * zat(k) + c, pick(k, across[1], across[2])]
        return copy(slot, slot, wx_s.at[w, k, 3], wx_r.at[w, k, 3], (dp, pick(k, across[2], across[1])))

    def w_c(w, k, j):
        slot = wbuf.at[w, 2 * zat(k) + c, whose(j)]
        return copy(slot, slot, wc_s.at[w, k, j], wc_r.at[w, k, j], core)

    def w_z_wait(w, k):
        slot = wbuf.at[w, 2 * zat(k) + c, m]
        copy(slot, slot, wz_s.at[w, k], wz_r.at[w, k], core).wait_recv()

    def w_x_wait(w, k, j):
        slot = wbuf.at[w, 2 * zat(k) + c, whose(j)]
        copy(slot, slot, wx_s.at[w, k, j], wx_r.at[w, k, j], core).wait_recv()

    def w_c_wait(w, k, j):
        slot = wbuf.at[w, 2 * zat(k) + other, whose(j)]
        copy(slot, slot, wc_s.at[w, k, j], wc_r.at[w, k, j], core).wait_recv()

    def w_start(w):
        for k in range(1, nz):
            w_z(w, k).start()
        wbuf[w, dp, m] = w_refs[w][...]
        for j in near:
            w_x(w, 0, j).start()
        w_c(w, 0, 0).start()

    def w_pass_z(w):
        def body(k):
            w_z_wait(w, k)
            for j in near:
                w_x(w, k, j).start()
            w_c(w, k, 0).start()

        loop(1, nz, body)

    def w_pass_x(w):
        def body(k):
            for j in near:
                w_x_wait(w, k, j)
                w_c(w, k, j).start()
            if square:
                w_diag(w, k).start()

        loop(0, nz, body)

    def join(w, d):
        for q in range(nm):
            fs[q * wrows:(q + 1) * wrows, :] = wbuf[w, d, q].astype(F32)
        wfull[w, pl.ds(pl.multiple_of(d * big, 16), big), :] = fs[...].astype(BF16)

    def w_finish(w):
        def own(k):
            if square:
                w_x_wait(w, k, 3)
                w_c(w, k, 3).start()
            if group == 1:
                join(w, 2 * zat(k) + c)

        loop(0, nz, own)

        def rest(k):
            for j in range(nm):
                w_c_wait(w, k, j)
            if group == 1:
                join(w, 2 * zat(k) + other)

        loop(0, nz, rest)

        def join_group(g):
            for n in range(group * nm):
                d = g * group + n // nm
                fs[n * wrows:(n + 1) * wrows, :] = wbuf[w, d, n % nm].astype(F32)
            wfull[w, pl.ds(pl.multiple_of(g * group * big, 16), group * big), :] = fs[...].astype(BF16)

        if group > 1:
            loop(0, 2 * nz // group, join_group)

    def embed(w):
        pre = dot(x_refs[w][...], wfull[w], 1, 0)
        radius = jnp.sqrt(jnp.sum(pre * pre, axis=1, keepdims=True) + 1e-06)
        out = pre / radius
        unit[w] = out
        rad[w] = radius
        return out.astype(BF16)

    def my(n):
        return pl.ds(pl.multiple_of(n * rows, rows), rows)

    def ids_img(j):
        return copy(iids.at[m], iids.at[m], ii_s.at[j], ii_r.at[j], (dp, mto(j)))

    def ids_txt(k):
        return copy(tids.at[dp], tids.at[dp], ti_s.at[k], ti_r.at[k], (2 * zto(k) + c, m))

    def ids_core(k):
        slot = tids.at[2 * zat(k) + c]
        return copy(slot, slot, tj_s.at[k], tj_r.at[k], core)

    def img_x(j):
        slot = imgs.at[my(m), :]
        return copy(slot, slot, im_s.at[j], im_r.at[j], (dp, mto(j)))

    def txt_z(k):
        slot = txts.at[my(dp), :]
        there = beyond(k) if line else zto(k)
        return copy(slot, slot, tx_s.at[k], tx_r.at[k], (2 * there + c, m))

    def txt_on():
        slot = txts.at[my(2 * beyond(2) + c), :]
        return copy(slot, slot, tx_s.at[3], tx_r.at[3], (2 * beyond(1) + c, m))

    def txt_c(k):
        slot = txts.at[my(2 * zof(k) + c), :]
        return copy(slot, slot, ty_s.at[k], ty_r.at[k], core)

    w_start(TXT)
    iids[m] = jnp.broadcast_to(idimg[...], (8, rows))
    tids[dp] = jnp.broadcast_to(idtxt[...], (8, rows))
    for j in range(1, nm):
        ids_img(j).start()
    for k in range(1, nz):
        ids_txt(k).start()
    ids_core(0).start()
    w_pass_z(TXT)
    w_start(IMG)
    w_pass_x(TXT)
    for k in range(1, nz):
        slot = tids.at[2 * zat(k) + c]
        copy(slot, slot, ti_s.at[k], ti_r.at[k], core).wait_recv()
        ids_core(k).start()
    for w in (TXT, IMG):
        turned = x_refs[w][...].T if group == 1 else x_refs[w][...].astype(F32).T
        for d in range(2 * nz):
            xt[w, d] = turned[d * big:(d + 1) * big, :].astype(BF16)
    w_pass_z(IMG)
    w_finish(TXT)
    txts[my(dp), :] = embed(TXT)
    for k in (2, 1) if line else range(1, nz):
        txt_z(k).start()
    txt_c(0).start()
    w_pass_x(IMG)
    w_finish(IMG)
    imgs[my(m), :] = embed(IMG)
    for j in range(1, nm):
        img_x(j).start()

    for k in (2, 1, 3) if line else range(1, nz):
        slot = txts.at[my(2 * zof(k) + c), :]
        copy(slot, slot, tx_s.at[k], tx_r.at[k], core).wait_recv()
        if line and k == 2:
            txt_on().start()
        txt_c(k).start()

    for j in range(1, nm):
        slot = iids.at[mat(j)]
        copy(slot, slot, ii_s.at[j], ii_r.at[j], core).wait_recv()
    for k in range(nz):
        slot = tids.at[2 * zat(k) + other]
        copy(slot, slot, tj_s.at[k], tj_r.at[k], core).wait_recv()
    for j in range(1, nm):
        slot = imgs.at[my(mat(j)), :]
        copy(slot, slot, im_s.at[j], im_r.at[j], core).wait_recv()

    sim, off = sim_ref[0], off_ref[0]

    def grad_core(k):
        return copy(tcs.at[k], tcr.at[k], tc_s.at[k], tc_r.at[k], core)

    def grad_z(k):
        there = pick(k, beyond(2), beyond(1)) if line else zat(k)
        return copy(tzs.at[k], tzr.at[k], tz_s.at[k], tz_r.at[k], (2 * there + c, m))

    def pair(i):
        if line:
            k = 3 - 2 * lax.div(i + 1, 2) + lax.div(i, 2)
        else:
            k = lax.rem(i + 1, nz)
        zs = zof(k)

        slot = txts.at[my(2 * zs + other), :]
        copy(slot, slot, ty_s.at[k], ty_r.at[k], core).wait_recv()
        span = pl.ds(pl.multiple_of(zs * 2 * rows, 2 * rows), 2 * rows)
        idrow = jnp.concatenate([tids[2 * zs][:1], tids[2 * zs + 1][:1]], axis=1)

        logits = sim * dot(imgs[...], txts[span, :], 1, 1) + off
        idcol = jnp.concatenate([iids[q].T[:, :1] for q in range(nm)], axis=0)
        sign = jnp.where(idcol == idrow, 1.0, -1.0).astype(F32)
        slope = (-sign * jax.nn.sigmoid(-sign * logits)).astype(BF16)
        slopes[:, span] = slope
        part = dot(slope, imgs[...], 0, 0)
        for h in range(2):
            dt[h] = part[h * rows:(h + 1) * rows, :]
        tcs[k] = dt[other].astype(BF16)
        grad_core(k).start()
        grad_core(k).wait_recv()

        gown[TXT] = dt[c] + tcr[k].astype(F32)
        if line:
            @pl.when(k == 2)
            def _():
                grad_z(3).wait_recv()
                gown[TXT] = gown[TXT] + tzr[3].astype(F32)

        @pl.when(k > 0)
        def _():
            tzs[k] = gown[TXT].astype(BF16)
            grad_z(k).start()

    loop(0, nz, pair)

    def grad_img(j):
        return copy(dis.at[j], dir_.at[j], di_s.at[j], di_r.at[j], (dp, mto(j)))

    def img_part(j):
        part = dot(slopes[my(mto(j)), :], txts[...], 1, 0)

        @pl.when(j < nm)
        def _():
            dis[j] = part.astype(BF16)
            grad_img(j).start()

        @pl.when(j == nm)
        def _():
            gown[IMG] = part

    loop(1, nm + 1, img_part)

    def rs_core(w, k):
        return copy(rcs.at[w, k], rcr.at[w, k], rc_s.at[w, k], rc_r.at[w, k], core)

    def rs_x(w, k):
        there = (dp, pick(k, across[1], across[2]))
        return copy(rxs.at[w, k, pl.ds(2, 2)], rxr.at[w, k], rx_s.at[w, k, 0], rx_r.at[w, k, 0], there)

    def rs_far(w, k, j):
        return copy(rxs.at[w, k, mto(j)], rxr.at[w, k, j], rx_s.at[w, k, j], rx_r.at[w, k, j], (dp, mto(j)))

    def rs_y(w, k):
        there = (dp, pick(k, across[2], across[1]))
        return copy(rys.at[w, k], ryr.at[w, k], rx_s.at[w, k, 1], rx_r.at[w, k, 1], there)

    def rs_z(w, k):
        return copy(rzs.at[w, k], rzr.at[w, k], rz_s.at[w, k], rz_r.at[w, k], (2 * zto(k) + c, m))

    def w_part(w, d):
        return dot(xt[w, d], dpre[w], 1, 0)

    def backward(w, grad):
        u = unit[w]
        d = (grad - u * jnp.sum(u * grad, axis=1, keepdims=True)) / rad[w]
        dpre[w] = d.astype(BF16)

        def body(i):
            k = lax.rem(i, nz)
            rcs[w, k] = w_part(w, 2 * zto(k) + other).astype(BF16)
            rs_core(w, k).start()

        loop(1, nz + 1, body)

    def to_mp(w):
        def body(i):
            k = lax.rem(i, nz)
            rs_core(w, k).wait_recv()
            fs[:big, :] = w_part(w, 2 * zto(k) + c) + rcr[w, k].astype(F32)
            for q in range(nm):
                dx, dy = lax.rem(xbit + q % 2, 2), lax.rem(ybit + q // 2, 2)
                place = pick(k, 2 * dx + dy, 2 * dy + dx) if square else q
                rxs[w, k, place] = fs[q * wrows:(q + 1) * wrows, :].astype(BF16)
            if square:
                rs_x(w, k).start()
            else:
                for j in near:
                    rs_far(w, k, j).start()

        loop(1, nz + 1, body)

    def to_y(w):
        def body(i):
            k = lax.rem(i, nz)
            rs_x(w, k).wait_recv()
            rys[w, k] = (rxs[w, k, 1].astype(F32) + rxr[w, k, 1].astype(F32)).astype(BF16)
            rs_y(w, k).start()

        if square:
            loop(1, nz + 1, body)

    def to_z(w):
        def body(i):
            k = lax.rem(i, nz)
            if square:
                rs_y(w, k).wait_recv()
                total = rxs[w, k, 0].astype(F32) + rxr[w, k, 0].astype(F32) + ryr[w, k].astype(F32)
            else:
                total = rxs[w, k, m].astype(F32)
                for j in near:
                    rs_far(w, k, j).wait_recv()
                    total = total + rxr[w, k, j].astype(F32)

            @pl.when(k > 0)
            def _():
                rzs[w, k] = total.astype(BF16)
                rs_z(w, k).start()

            @pl.when(k == 0)
            def _():
                rown[w] = total

        loop(1, nz + 1, body)

    def finish(w, out):
        total = rown[w]
        for k in range(1, nz):
            rs_z(w, k).wait_recv()
            total = total + rzr[w, k].astype(F32)
        out[...] = total

    grad = gown[IMG]
    for j in range(1, nm):
        grad_img(j).wait_recv()
        grad = grad + dir_[j].astype(F32)
    backward(IMG, sim * grad)
    gimg[...] = dot(dpre[IMG], wfull[IMG], 1, 1).astype(BF16)
    to_mp(IMG)
    to_y(IMG)
    grad = gown[TXT]
    for k in (1, 2) if line else range(1, nz):
        grad_z(k).wait_recv()
        grad = grad + tzr[k].astype(F32)
    backward(TXT, sim * grad)
    to_mp(TXT)
    to_z(IMG)
    to_y(TXT)
    gtxt[...] = dot(dpre[TXT], wfull[TXT], 1, 1).astype(BF16)
    to_z(TXT)
    finish(IMG, dwimg)
    finish(TXT, dwtxt)

    for k in range(nz):
        ids_core(k).wait_send()
        txt_c(k).wait_send()
        grad_core(k).wait_send()
        if k > 0:
            ids_txt(k).wait_send()
            if line and k == 3:
                txt_on().wait_send()
            else:
                txt_z(k).wait_send()
            grad_z(k).wait_send()
    for j in range(1, nm):
        ids_img(j).wait_send()
        img_x(j).wait_send()
        grad_img(j).wait_send()
    for w in (TXT, IMG):
        def body(k):
            for j in range(nm):
                w_c(w, k, j).wait_send()
            rs_core(w, k).wait_send()
            for j in near:
                w_x(w, k, j).wait_send()
            if square:
                w_diag(w, k).wait_send()
                rs_x(w, k).wait_send()
                rs_y(w, k).wait_send()
            else:
                for j in near:
                    rs_far(w, k, j).wait_send()

            @pl.when(k > 0)
            def _():
                w_z(w, k).wait_send()
                rs_z(w, k).wait_send()

        loop(0, nz, body)


def call(nz, nm, args):
    ximg, xtxt, wimg, wtxt, idimg, idtxt, sim, off = args
    rows, depth = ximg.shape
    wrows, width = wimg.shape
    big = nm * wrows
    ndp = 2 * nz
    dma = pltpu.SemaphoreType.DMA
    vm = pltpu.VMEM
    sems = [
        dma((2, nz)), dma((2, nz)), dma((2, nz, nm)), dma((2, nz, nm)), dma((2, nz, nm)), dma((2, nz, nm)),
        dma((nm,)), dma((nm,)), dma((nz,)), dma((nz,)), dma((nz,)), dma((nz,)),
        dma((nm,)), dma((nm,)), dma((nz,)), dma((nz,)), dma((nz,)), dma((nz,)),
        dma((nz,)), dma((nz,)), dma((nz,)), dma((nz,)), dma((nm,)), dma((nm,)),
        dma((2, nz)), dma((2, nz)), dma((2, nz, nm)), dma((2, nz, nm)), dma((2, nz)), dma((2, nz)),
    ]
    scratch = [
        vm((2, ndp, nm, wrows, width), BF16),
        vm((2, depth, width), BF16),
        vm((math.lcm(big, 16), width), F32),
        vm((2, ndp, big, rows), BF16),
        vm((2, rows, width), F32),
        vm((2, rows, 1), F32),
        vm((2, rows, width), BF16),
        vm((nm * rows, width), BF16),
        vm((ndp * rows, width), BF16),
        vm((nm, 8, rows), jnp.int32),
        vm((ndp, 8, rows), jnp.int32),
        vm((nm * rows, ndp * rows), BF16),
        vm((2, rows, width), F32),
        vm((nz, rows, width), BF16),
        vm((nz, rows, width), BF16),
        vm((nz, rows, width), BF16),
        vm((nz, rows, width), BF16),
        vm((nm, rows, width), BF16),
        vm((nm, rows, width), BF16),
        vm((2, rows, width), F32),
        vm((2, nz, big, width), BF16),
        vm((2, nz, big, width), BF16),
        vm((2, nz, nm, wrows, width), BF16),
        vm((2, nz, 2 if nm == 4 else nm, wrows, width), BF16),
        vm((2, nz, wrows, width), BF16),
        vm((2, nz, wrows, width), BF16),
        vm((2, nz, wrows, width), BF16),
        vm((2, nz, wrows, width), BF16),
        vm((2, wrows, width), F32),
    ]
    whole = pl.BlockSpec(memory_space=pltpu.VMEM)
    scalar = pl.BlockSpec(memory_space=pltpu.SMEM)
    return pl.pallas_call(
        functools.partial(kernel, nz, nm, rows, wrows),
        out_shape=(
            jax.ShapeDtypeStruct((rows, depth), BF16),
            jax.ShapeDtypeStruct((rows, depth), BF16),
            jax.ShapeDtypeStruct((wrows, width), F32),
            jax.ShapeDtypeStruct((wrows, width), F32),
        ),
        in_specs=[whole] * 6 + [scalar] * 2,
        out_specs=(whole,) * 4,
        scratch_shapes=scratch + sems,
        compiler_params=pltpu.CompilerParams(
            collective_id=0, has_side_effects=True, vmem_limit_bytes=62 * 1024 * 1024
        ),
        cost_estimate=pl.CostEstimate(flops=6 * 10**9, bytes_accessed=4 * 10**6, transcendentals=0),
    )(
        ximg, xtxt, wimg, wtxt,
        idimg[None, :], idtxt[None, :],
        sim, off,
    )


def solution(mesh):
    ndp, nm = mesh.shape["dp"], mesh.shape["mp"]

    def on_device(*args):
        return call(ndp // 2, nm, args)

    spec = P(("dp", "mp"), None)
    ids = P(("dp", "mp"))
    return jax.shard_map(
        on_device,
        mesh=mesh,
        in_specs=(spec, spec, spec, spec, ids, ids, P(), P()),
        out_specs=(spec,) * 4,
        check_vma=False,
    )
```

```python
import functools
import math

import jax
import jax.numpy as jnp
from jax import lax
from jax.experimental import pallas as pl
from jax.experimental.pallas import tpu as pltpu
from jax.sharding import PartitionSpec as P

MESH = pl.DeviceIdType.MESH
TXT, IMG = 0, 1
F32, BF16 = jnp.float32, jnp.bfloat16


def dot(a, b, da, db):
    return lax.dot_general(a, b, (((da,), (db,)), ((), ())), preferred_element_type=F32)


def loop(low, high, body):
    def step(i, carry):
        body(i)
        return carry

    lax.fori_loop(low, high, step, 0)


def kernel(
    nz, nm, rows, wrows,
    ximg, xtxt, wimg, wtxt, idimg, idtxt, sim_ref, off_ref,
    gimg, gtxt, dwimg, dwtxt,
    wbuf, wfull, fs, xt, unit, rad, dpre, imgs, txts, iids, tids, slopes,
    dt, tcs, tcr, tzs, tzr, dis, dir_, gown,
    rcs, rcr, rxs, rxr, rys, ryr, rzs, rzr, rown,
    wz_s, wz_r, wx_s, wx_r, wc_s, wc_r,
    ii_s, ii_r, ti_s, ti_r, tj_s, tj_r,
    im_s, im_r, tx_s, tx_r, ty_s, ty_r,
    tc_s, tc_r, tz_s, tz_r, di_s, di_r,
    rc_s, rc_r, rx_s, rx_r, rz_s, rz_r,
):
    dp, m = lax.axis_index("dp"), lax.axis_index("mp")
    z, c = lax.div(dp, 2), lax.rem(dp, 2)
    other = 1 - c
    big = nm * wrows
    group = fs.shape[0] // big
    x_refs, w_refs = (xtxt, ximg), (wtxt, wimg)

    def zat(k):
        return lax.rem(z - k + nz, nz)

    def zto(k):
        return lax.rem(z + k, nz)

    def mat(k):
        return lax.rem(m - k + nm, nm)

    def mto(k):
        return lax.rem(m + k, nm)

    core = (2 * z + other, m)
    square = nm == 4
    xbit, ybit = lax.rem(m, 2), lax.div(m, 2)
    across = (m, m + 1 - 2 * xbit, m + 2 - 4 * ybit, 3 - m)
    near = (1, 2) if square else range(1, nm)

    def whom(j):
        return across[j] if square else mto(j)

    def whose(j):
        return across[j] if square else mat(j)

    def pick(k, even, odd):
        return even + lax.rem(k, 2) * (odd - even)

    def copy(src, dst, s, r, dev):
        return pltpu.make_async_remote_copy(
            src_ref=src, dst_ref=dst, send_sem=s, recv_sem=r, device_id=dev, device_id_type=MESH
        )

    barrier = pltpu.get_barrier_semaphore()
    for k in range(1, nz):
        pl.semaphore_signal(barrier, inc=1, device_id=(2 * zto(k) + c, m), device_id_type=MESH)
    for k in range(1, nm):
        pl.semaphore_signal(barrier, inc=1, device_id=(dp, mto(k)), device_id_type=MESH)
    pl.semaphore_signal(barrier, inc=1, device_id=core, device_id_type=MESH)
    pl.semaphore_wait(barrier, nz + nm - 1)

    def w_z(w, k):
        return copy(w_refs[w], wbuf.at[w, dp, m], wz_s.at[w, k], wz_r.at[w, k], (2 * zto(k) + c, m))

    def w_x(w, k, j):
        slot = wbuf.at[w, 2 * zat(k) + c, m]
        return copy(slot, slot, wx_s.at[w, k, j], wx_r.at[w, k, j], (dp, whom(j)))

    def w_diag(w, k):
        slot = wbuf.at[w, 2 * zat(k) + c, pick(k, across[1], across[2])]
        return copy(slot, slot, wx_s.at[w, k, 3], wx_r.at[w, k, 3], (dp, pick(k, across[2], across[1])))

    def w_c(w, k):
        slot = wbuf.at[w, 2 * zat(k) + c]
        return copy(slot, slot, wc_s.at[w, k], wc_r.at[w, k], core)

    def w_z_wait(w, k):
        slot = wbuf.at[w, 2 * zat(k) + c, m]
        copy(slot, slot, wz_s.at[w, k], wz_r.at[w, k], core).wait_recv()

    def w_x_wait(w, k, j):
        slot = wbuf.at[w, 2 * zat(k) + c, whose(j)]
        copy(slot, slot, wx_s.at[w, k, j], wx_r.at[w, k, j], core).wait_recv()

    def w_c_wait(w, k):
        slot = wbuf.at[w, 2 * zat(k) + other]
        copy(slot, slot, wc_s.at[w, k], wc_r.at[w, k], core).wait_recv()

    def w_start(w):
        for k in range(1, nz):
            w_z(w, k).start()
        wbuf[w, dp, m] = w_refs[w][...]
        for j in near:
            w_x(w, 0, j).start()

    def w_pass_z(w):
        def body(k):
            w_z_wait(w, k)
            for j in near:
                w_x(w, k, j).start()

        loop(1, nz, body)

    def w_pass_x(w):
        def body(k):
            for j in near:
                w_x_wait(w, k, j)
            if square:
                w_diag(w, k).start()

        loop(0, nz, body)

    def join(w, d):
        for q in range(nm):
            fs[q * wrows:(q + 1) * wrows, :] = wbuf[w, d, q].astype(F32)
        wfull[w, pl.ds(pl.multiple_of(d * big, 16), big), :] = fs[...].astype(BF16)

    def w_finish(w):
        def own(k):
            if square:
                w_x_wait(w, k, 3)
            w_c(w, k).start()
            if group == 1:
                join(w, 2 * zat(k) + c)

        loop(0, nz, own)

        def rest(k):
            w_c_wait(w, k)
            if group == 1:
                join(w, 2 * zat(k) + other)

        loop(0, nz, rest)

        def join_group(g):
            for n in range(group * nm):
                d = g * group + n // nm
                fs[n * wrows:(n + 1) * wrows, :] = wbuf[w, d, n % nm].astype(F32)
            wfull[w, pl.ds(pl.multiple_of(g * group * big, 16), group * big), :] = fs[...].astype(BF16)

        if group > 1:
            loop(0, 2 * nz // group, join_group)

    def embed(w):
        pre = dot(x_refs[w][...], wfull[w], 1, 0)
        radius = jnp.sqrt(jnp.sum(pre * pre, axis=1, keepdims=True) + 1e-06)
        out = pre / radius
        unit[w] = out
        rad[w] = radius
        return out.astype(BF16)

    def my(n):
        return pl.ds(pl.multiple_of(n * rows, rows), rows)

    def ids_img(j):
        return copy(iids.at[m], iids.at[m], ii_s.at[j], ii_r.at[j], (dp, mto(j)))

    def ids_txt(k):
        return copy(tids.at[dp], tids.at[dp], ti_s.at[k], ti_r.at[k], (2 * zto(k) + c, m))

    def ids_core(k):
        slot = tids.at[2 * zat(k) + c]
        return copy(slot, slot, tj_s.at[k], tj_r.at[k], core)

    def img_x(j):
        slot = imgs.at[my(m), :]
        return copy(slot, slot, im_s.at[j], im_r.at[j], (dp, mto(j)))

    def txt_z(k):
        slot = txts.at[my(dp), :]
        return copy(slot, slot, tx_s.at[k], tx_r.at[k], (2 * zto(k) + c, m))

    def txt_c(k):
        slot = txts.at[my(2 * zat(k) + c), :]
        return copy(slot, slot, ty_s.at[k], ty_r.at[k], core)

    w_start(TXT)
    iids[m] = jnp.broadcast_to(idimg[...], (8, rows))
    tids[dp] = jnp.broadcast_to(idtxt[...], (8, rows))
    for j in range(1, nm):
        ids_img(j).start()
    for k in range(1, nz):
        ids_txt(k).start()
    ids_core(0).start()
    w_pass_z(TXT)
    w_start(IMG)
    w_pass_x(TXT)
    for k in range(1, nz):
        slot = tids.at[2 * zat(k) + c]
        copy(slot, slot, ti_s.at[k], ti_r.at[k], core).wait_recv()
        ids_core(k).start()
    for w in (TXT, IMG):
        turned = x_refs[w][...].T if group == 1 else x_refs[w][...].astype(F32).T
        for d in range(2 * nz):
            xt[w, d] = turned[d * big:(d + 1) * big, :].astype(BF16)
    w_pass_z(IMG)
    w_finish(TXT)
    txts[my(dp), :] = embed(TXT)
    for k in range(1, nz):
        txt_z(k).start()
    txt_c(0).start()
    w_pass_x(IMG)
    w_finish(IMG)
    imgs[my(m), :] = embed(IMG)
    for j in range(1, nm):
        img_x(j).start()

    def take_txt(k):
        slot = txts.at[my(2 * zat(k) + c), :]
        copy(slot, slot, tx_s.at[k], tx_r.at[k], core).wait_recv()
        txt_c(k).start()

    loop(1, nz, take_txt)
    for j in range(1, nm):
        slot = iids.at[mat(j)]
        copy(slot, slot, ii_s.at[j], ii_r.at[j], core).wait_recv()
    for k in range(nz):
        slot = tids.at[2 * zat(k) + other]
        copy(slot, slot, tj_s.at[k], tj_r.at[k], core).wait_recv()
    for j in range(1, nm):
        slot = imgs.at[my(mat(j)), :]
        copy(slot, slot, im_s.at[j], im_r.at[j], core).wait_recv()

    sim, off = sim_ref[0], off_ref[0]

    def grad_core(k):
        return copy(tcs.at[k], tcr.at[k], tc_s.at[k], tc_r.at[k], core)

    def grad_z(k):
        return copy(tzs.at[k], tzr.at[k], tz_s.at[k], tz_r.at[k], (2 * zat(k) + c, m))

    def pair(i):
        k = lax.rem(i, nz)
        zs = zat(k)

        slot = txts.at[my(2 * zs + other), :]
        copy(slot, slot, ty_s.at[k], ty_r.at[k], core).wait_recv()
        span = pl.ds(pl.multiple_of(zs * 2 * rows, 2 * rows), 2 * rows)
        idrow = jnp.concatenate([tids[2 * zs][:1], tids[2 * zs + 1][:1]], axis=1)

        logits = sim * dot(imgs[...], txts[span, :], 1, 1) + off
        idcol = jnp.concatenate([iids[q].T[:, :1] for q in range(nm)], axis=0)
        sign = jnp.where(idcol == idrow, 1.0, -1.0).astype(F32)
        slope = (-sign * jax.nn.sigmoid(-sign * logits)).astype(BF16)
        slopes[:, span] = slope
        part = dot(slope, imgs[...], 0, 0)
        turn = lax.rem(k, 2)
        for h in range(2):
            @pl.when(c == h)
            def _():
                dt[turn] = part[h * rows:(h + 1) * rows, :]
                tcs[k] = part[(1 - h) * rows:(2 - h) * rows, :].astype(BF16)

        grad_core(k).start()

        @pl.when(i > 1)
        def _():
            sum_core(i - 1)

    def sum_core(k):
        grad_core(k).wait_recv()
        tzs[k] = (dt[lax.rem(k, 2)] + tcr[k].astype(F32)).astype(BF16)
        grad_z(k).start()

    loop(1, nz + 1, pair)

    def grad_img(j):
        return copy(dis.at[j], dir_.at[j], di_s.at[j], di_r.at[j], (dp, mto(j)))

    def img_part(j):
        part = dot(slopes[my(mto(j)), :], txts[...], 1, 0)

        @pl.when(j < nm)
        def _():
            dis[j] = part.astype(BF16)
            grad_img(j).start()

        @pl.when(j == nm)
        def _():
            gown[IMG] = part

    loop(1, nm + 1, img_part)
    grad_core(0).wait_recv()
    gown[TXT] = dt[0] + tcr[0].astype(F32)

    def rs_core(w, k):
        return copy(rcs.at[w, k], rcr.at[w, k], rc_s.at[w, k], rc_r.at[w, k], core)

    def rs_x(w, k):
        there = (dp, pick(k, across[1], across[2]))
        return copy(rxs.at[w, k, pl.ds(2, 2)], rxr.at[w, k], rx_s.at[w, k, 0], rx_r.at[w, k, 0], there)

    def rs_far(w, k, j):
        return copy(rxs.at[w, k, mto(j)], rxr.at[w, k, j], rx_s.at[w, k, j], rx_r.at[w, k, j], (dp, mto(j)))

    def rs_y(w, k):
        there = (dp, pick(k, across[2], across[1]))
        return copy(rys.at[w, k], ryr.at[w, k], rx_s.at[w, k, 1], rx_r.at[w, k, 1], there)

    def rs_z(w, k):
        return copy(rzs.at[w, k], rzr.at[w, k], rz_s.at[w, k], rz_r.at[w, k], (2 * zto(k) + c, m))

    def w_part(w, d):
        return dot(xt[w, d], dpre[w], 1, 0)

    def backward(w, grad):
        u = unit[w]
        d = (grad - u * jnp.sum(u * grad, axis=1, keepdims=True)) / rad[w]
        dpre[w] = d.astype(BF16)

        def body(i):
            k = lax.rem(i, nz)
            rcs[w, k] = w_part(w, 2 * zto(k) + other).astype(BF16)
            rs_core(w, k).start()

        loop(1, nz + 1, body)

    def to_mp(w):
        def body(i):
            k = lax.rem(i, nz)
            rs_core(w, k).wait_recv()
            fs[:big, :] = w_part(w, 2 * zto(k) + c) + rcr[w, k].astype(F32)
            for q in range(nm):
                dx, dy = lax.rem(xbit + q % 2, 2), lax.rem(ybit + q // 2, 2)
                place = pick(k, 2 * dx + dy, 2 * dy + dx) if square else q
                rxs[w, k, place] = fs[q * wrows:(q + 1) * wrows, :].astype(BF16)
            if square:
                rs_x(w, k).start()
            else:
                for j in near:
                    rs_far(w, k, j).start()

        loop(1, nz + 1, body)

    def to_y(w):
        def body(i):
            k = lax.rem(i, nz)
            rs_x(w, k).wait_recv()
            rys[w, k] = (rxs[w, k, 1].astype(F32) + rxr[w, k, 1].astype(F32)).astype(BF16)
            rs_y(w, k).start()

        if square:
            loop(1, nz + 1, body)

    def to_z(w):
        def body(i):
            k = lax.rem(i, nz)
            if square:
                rs_y(w, k).wait_recv()
                total = rxs[w, k, 0].astype(F32) + rxr[w, k, 0].astype(F32) + ryr[w, k].astype(F32)
            else:
                total = rxs[w, k, m].astype(F32)
                for j in near:
                    rs_far(w, k, j).wait_recv()
                    total = total + rxr[w, k, j].astype(F32)

            @pl.when(k > 0)
            def _():
                rzs[w, k] = total.astype(BF16)
                rs_z(w, k).start()

            @pl.when(k == 0)
            def _():
                rown[w] = total

        loop(1, nz + 1, body)

    def finish(w, out):
        total = rown[w]
        for k in range(1, nz):
            rs_z(w, k).wait_recv()
            total = total + rzr[w, k].astype(F32)
        out[...] = total

    grad = gown[IMG]
    for j in range(1, nm):
        grad_img(j).wait_recv()
        grad = grad + dir_[j].astype(F32)
    backward(IMG, sim * grad)
    grad = gown[TXT]
    for k in range(1, nz):
        grad_z(k).wait_recv()
        grad = grad + tzr[k].astype(F32)
    backward(TXT, sim * grad)
    to_mp(IMG)
    to_mp(TXT)
    gimg[...] = dot(dpre[IMG], wfull[IMG], 1, 1).astype(BF16)
    to_y(IMG)
    to_y(TXT)
    gtxt[...] = dot(dpre[TXT], wfull[TXT], 1, 1).astype(BF16)
    to_z(IMG)
    to_z(TXT)
    finish(IMG, dwimg)
    finish(TXT, dwtxt)

    for k in range(nz):
        ids_core(k).wait_send()
        txt_c(k).wait_send()
        grad_core(k).wait_send()
        if k > 0:
            ids_txt(k).wait_send()
            txt_z(k).wait_send()
            grad_z(k).wait_send()
    for j in range(1, nm):
        ids_img(j).wait_send()
        img_x(j).wait_send()
        grad_img(j).wait_send()
    for w in (TXT, IMG):
        def body(k):
            w_c(w, k).wait_send()
            rs_core(w, k).wait_send()
            for j in near:
                w_x(w, k, j).wait_send()
            if square:
                w_diag(w, k).wait_send()
                rs_x(w, k).wait_send()
                rs_y(w, k).wait_send()
            else:
                for j in near:
                    rs_far(w, k, j).wait_send()

            @pl.when(k > 0)
            def _():
                w_z(w, k).wait_send()
                rs_z(w, k).wait_send()

        loop(0, nz, body)


def call(nz, nm, args):
    ximg, xtxt, wimg, wtxt, idimg, idtxt, sim, off = args
    rows, depth = ximg.shape
    wrows, width = wimg.shape
    big = nm * wrows
    ndp = 2 * nz
    dma = pltpu.SemaphoreType.DMA
    vm = pltpu.VMEM
    sems = [
        dma((2, nz)), dma((2, nz)), dma((2, nz, nm)), dma((2, nz, nm)), dma((2, nz)), dma((2, nz)),
        dma((nm,)), dma((nm,)), dma((nz,)), dma((nz,)), dma((nz,)), dma((nz,)),
        dma((nm,)), dma((nm,)), dma((nz,)), dma((nz,)), dma((nz,)), dma((nz,)),
        dma((nz,)), dma((nz,)), dma((nz,)), dma((nz,)), dma((nm,)), dma((nm,)),
        dma((2, nz)), dma((2, nz)), dma((2, nz, nm)), dma((2, nz, nm)), dma((2, nz)), dma((2, nz)),
    ]
    scratch = [
        vm((2, ndp, nm, wrows, width), BF16),
        vm((2, depth, width), BF16),
        vm((math.lcm(big, 16), width), F32),
        vm((2, ndp, big, rows), BF16),
        vm((2, rows, width), F32),
        vm((2, rows, 1), F32),
        vm((2, rows, width), BF16),
        vm((nm * rows, width), BF16),
        vm((ndp * rows, width), BF16),
        vm((nm, 8, rows), jnp.int32),
        vm((ndp, 8, rows), jnp.int32),
        vm((nm * rows, ndp * rows), BF16),
        vm((2, rows, width), F32),
        vm((nz, rows, width), BF16),
        vm((nz, rows, width), BF16),
        vm((nz, rows, width), BF16),
        vm((nz, rows, width), BF16),
        vm((nm, rows, width), BF16),
        vm((nm, rows, width), BF16),
        vm((2, rows, width), F32),
        vm((2, nz, big, width), BF16),
        vm((2, nz, big, width), BF16),
        vm((2, nz, nm, wrows, width), BF16),
        vm((2, nz, 2 if nm == 4 else nm, wrows, width), BF16),
        vm((2, nz if nm == 4 else 1, wrows, width), BF16),
        vm((2, nz if nm == 4 else 1, wrows, width), BF16),
        vm((2, nz, wrows, width), BF16),
        vm((2, nz, wrows, width), BF16),
        vm((2, wrows, width), F32),
    ]
    whole = pl.BlockSpec(memory_space=pltpu.VMEM)
    scalar = pl.BlockSpec(memory_space=pltpu.SMEM)
    return pl.pallas_call(
        functools.partial(kernel, nz, nm, rows, wrows),
        out_shape=(
            jax.ShapeDtypeStruct((rows, depth), BF16),
            jax.ShapeDtypeStruct((rows, depth), BF16),
            jax.ShapeDtypeStruct((wrows, width), F32),
            jax.ShapeDtypeStruct((wrows, width), F32),
        ),
        in_specs=[whole] * 6 + [scalar] * 2,
        out_specs=(whole,) * 4,
        scratch_shapes=scratch + sems,
        compiler_params=pltpu.CompilerParams(
            collective_id=0, has_side_effects=True, vmem_limit_bytes=63 * 1024 * 1024
        ),
        cost_estimate=pl.CostEstimate(flops=6 * 10**9, bytes_accessed=4 * 10**6, transcendentals=0),
    )(
        ximg, xtxt, wimg, wtxt,
        idimg[None, :], idtxt[None, :],
        sim, off,
    )


def solution(mesh):
    ndp, nm = mesh.shape["dp"], mesh.shape["mp"]

    def on_device(*args):
        return call(ndp // 2, nm, args)

    spec = P(("dp", "mp"), None)
    ids = P(("dp", "mp"))
    return jax.shard_map(
        on_device,
        mesh=mesh,
        in_specs=(spec, spec, spec, spec, ids, ids, P(), P()),
        out_specs=(spec,) * 4,
        check_vma=False,
    )
```
